256 devices in a mesh: dp: 16 (over x, y), mp: 16 (over z, core).
Axes of the slice: x: 4, y: 4, z: 8, core: 2. Of those that a mesh axis runs over, the one named last changes fastest.
Arguments:
- tokens: bfloat16 [2048, 8192], P('dp', 'mp'), may hold values from -6 to 6
- gate_tiles: bfloat16 [65536, 128], P('mp'), may hold values from -0.3125 to 0.3125
- gate_index: int32 [2048, 2], P('mp'), may hold values from 0 to 223, as said below
- gate_count: int32 [256], P('mp'), may hold values from 1 to 8, as said below
- up_tiles: bfloat16 [65536, 128], P('mp'), may hold values from -0.3125 to 0.3125
- up_index: int32 [2048, 2], P('mp'), may hold values from 0 to 223, as said below
- up_count: int32 [256], P('mp'), may hold values from 1 to 8, as said below
- down_tiles: bfloat16 [65536, 128], P('mp'), may hold values from -0.25 to 0.25
- down_index: int32 [2048, 2], P('mp'), may hold values from 0 to 223, as said below
- down_count: int32 [256], P('mp'), may hold values from 1 to 8, as said below
- grad_output: bfloat16 [2048, 8192], P('dp', 'mp'), may hold values from -6 to 6
Outputs:
- layer_output: bfloat16 [2048, 8192], P('dp', 'mp')
- grad_tokens: bfloat16 [2048, 8192], P('dp', 'mp')
- grad_gate: bfloat16 [65536, 128], P('mp')
- grad_up: bfloat16 [65536, 128], P('mp')
- grad_down: bfloat16 [65536, 128], P('mp')
The draws below stay inside these ranges and needn't reach their ends.
Inputs may be any that keep to these rules, and one draw needn't show every extreme that they name: In each of gate_index and up_index, entry k = (q * 16 + e) * 8 + c has its row block (column 0) among q * 8 to (q + 1) * 8 - 1 and its column block (column 1) among e * 14 to (e + 1) * 14 - 1; the 128 entries of one q name distinct blocks. `up_index`: as for gate_index, drawn apart. `down_index`: entry k = (q * 16 + e) * 8 + c has its row block (column 0) among q * 14 to (q + 1) * 14 - 1 of the hidden blocks and its column block (column 1) among e * 8 to (e + 1) * 8 - 1; the 128 entries of one q name distinct blocks. `gate_count`: some e has count 8 from every q. `up_count`: some e has count 8 from every q. `down_count`: some e has count 8 from every q.
All inputs are finite; a program needn't handle non-finite values.
Results may differ from the reference program's by a relative error of at most 0.03.
Values may be sent and summed in bfloat16 or wider, within the bound.
No kernel may reach another device: no remote copies, remote signals or barrier semaphores. Data moves between devices by JAX's collectives and lax.ppermute only.
A program may use at most 128 MiB of HBM per device.

```python
import jax
import jax.numpy as jnp
from jax import lax

D = 8192
FF = 14336
TILE = 64
CAP = 8
TOK_DEV = 128
TOKENS = 2048
D_BLK = 128
F_BLK = 224
D_OWN = 8
F_OWN = 14
NTILES = 2048
N_DP = 16
N_MP = 16


def tile_pattern(key, row_own, col_own):
    buckets = N_MP * N_MP
    bucket_keys = jax.random.split(jax.random.fold_in(key, 11), buckets)
    positions = jax.vmap(lambda item: jax.random.permutation(item, row_own * col_own)[:CAP])(bucket_keys)
    positions = positions.astype(jnp.int32)
    source = (jnp.arange(buckets, dtype=jnp.int32) // N_MP)[:, None]
    target = (jnp.arange(buckets, dtype=jnp.int32) % N_MP)[:, None]
    rows_global = source * row_own + positions // col_own
    cols_global = target * col_own + positions % col_own
    index_list = jnp.stack([rows_global, cols_global], axis=-1).reshape(buckets * CAP, 2).astype(jnp.int32)
    count_list = jax.random.randint(jax.random.fold_in(key, 12), (buckets,), 1, CAP + 1).astype(jnp.int32)
    busiest = jax.random.randint(jax.random.fold_in(key, 13), (), 0, N_MP).astype(jnp.int32)
    count_list = jnp.where(target[:, 0] == busiest, CAP, count_list).astype(jnp.int32)
    return (index_list, count_list)


def draw_gate_index(key, part):
    shared_key = jax.random.fold_in(key, 101)
    return tile_pattern(shared_key, D_OWN, F_OWN)[0]


def draw_gate_count(key, part):
    shared_key = jax.random.fold_in(key, 101)
    return tile_pattern(shared_key, D_OWN, F_OWN)[1]


def draw_up_index(key, part):
    shared_key = jax.random.fold_in(key, 102)
    return tile_pattern(shared_key, D_OWN, F_OWN)[0]


def draw_up_count(key, part):
    shared_key = jax.random.fold_in(key, 102)
    return tile_pattern(shared_key, D_OWN, F_OWN)[1]


def draw_down_index(key, part):
    shared_key = jax.random.fold_in(key, 103)
    return tile_pattern(shared_key, F_OWN, D_OWN)[0]


def draw_down_count(key, part):
    shared_key = jax.random.fold_in(key, 103)
    return tile_pattern(shared_key, F_OWN, D_OWN)[1]


def level_of(own_key, extent, pieces, low, high):
    factor_of, own = 1.0, jax.random.fold_in(own_key, 6)
    for position, parts in pieces:
        steps = jnp.exp(jax.random.uniform(jax.random.fold_in(own, position), (parts,), jnp.float32, low / len(pieces), high / len(pieces)))
        factor_of = factor_of * jnp.repeat(steps, extent[position] // parts).reshape([-1 if axis == position else 1 for axis in range(len(extent))])
    return factor_of


def centred(rng, shape, width, reach, pieces=(), kind=jnp.bfloat16):
    result = width * jax.random.normal(rng, shape, jnp.float32)
    if pieces:
        result = result * level_of(rng, shape, pieces, -0.22, 0.18)
    return jnp.clip(result, -reach, reach).astype(kind)


def setup_inputs(seed: int = 0) -> dict:
    keys = jax.random.split(jax.random.key(seed), 12)
    return {
        "tokens": centred(keys[0], (TOKENS, D), 1.0, 6.0, ((0, 16), (1, 16))),
        "gate_tiles": centred(keys[1], (NTILES * TILE // 2, 2 * TILE), (TILE * D_BLK * (CAP + 1) // (2 * D_OWN * F_OWN)) ** -0.5, 0.3125, ((0, 16),)),
        "gate_index": draw_gate_index(jax.random.fold_in(keys[11], 71), 0),
        "gate_count": draw_gate_count(jax.random.fold_in(keys[11], 71), 0),
        "up_tiles": centred(keys[4], (NTILES * TILE // 2, 2 * TILE), (TILE * D_BLK * (CAP + 1) // (2 * D_OWN * F_OWN)) ** -0.5, 0.3125, ((0, 16),)),
        "up_index": draw_up_index(jax.random.fold_in(keys[11], 71), 0),
        "up_count": draw_up_count(jax.random.fold_in(keys[11], 71), 0),
        "down_tiles": centred(keys[7], (NTILES * TILE // 2, 2 * TILE), (TILE * F_BLK * (CAP + 1) // (2 * D_OWN * F_OWN)) ** -0.5, 0.25, ((0, 16),)),
        "down_index": draw_down_index(jax.random.fold_in(keys[11], 71), 0),
        "down_count": draw_down_count(jax.random.fold_in(keys[11], 71), 0),
        "grad_output": centred(keys[10], (TOKENS, D), 1.0, 6.0, ((0, 16), (1, 16))),
    }


HIGH = lax.Precision.HIGHEST

def rounded(values):
    return values.astype(jnp.bfloat16).astype(jnp.float32)

def select_ref(values, hot_table, shared):
    if shared:
        form = 'tri,gcr->tgci'
    else:
        form = 'tgri,gcr->tgci'
    return jnp.einsum(form, values.astype(jnp.float32), hot_table, precision=HIGH)

def place_ref(product, hot_table, shared):
    if shared:
        form = 'tgci,gcr->tri'
    else:
        form = 'tgci,gcr->tgri'
    return jnp.einsum(form, product, hot_table, precision=HIGH)

def forward_ref(left_rows, left_shared, tile_values, row_table, col_table, out_shared):
    picked = select_ref(left_rows, row_table, left_shared)
    product = jnp.einsum('tgci,gcij->tgcj', picked, tile_values.astype(jnp.float32), precision=HIGH)
    return place_ref(product, col_table, out_shared)

def backward_ref(right_rows, right_shared, tile_values, row_table, col_table, out_shared):
    picked = select_ref(right_rows, col_table, right_shared)
    product = jnp.einsum('tgcj,gcij->tgci', picked, tile_values.astype(jnp.float32), precision=HIGH)
    return place_ref(product, row_table, out_shared)

def grads_ref(left_rows, left_shared, right_rows, right_shared, row_table, col_table):
    left_picked = select_ref(left_rows, row_table, left_shared)
    right_picked = select_ref(right_rows, col_table, right_shared)
    return jnp.einsum('tgci,tgcj->gcij', left_picked, right_picked, precision=HIGH)

def tables_ref(index_list, count_list, row_size, col_size):
    blocks = index_list.reshape(N_MP, N_MP, CAP, 2)
    owners = jnp.arange(N_MP, dtype=jnp.int32)
    rows_local = blocks[..., 0] - owners[:, None, None] * row_size
    cols_local = blocks[..., 1] - owners[None, :, None] * col_size
    valid_mask = (jnp.arange(CAP, dtype=jnp.int32)[None, None, :] < count_list.reshape(N_MP, N_MP)[..., None]).astype(jnp.float32)
    row_table = (rows_local[..., None] == jnp.arange(row_size, dtype=jnp.int32)).astype(jnp.float32) * valid_mask[..., None]
    col_table = (cols_local[..., None] == jnp.arange(col_size, dtype=jnp.int32)).astype(jnp.float32)
    return (row_table, col_table)

def replica_sum(left_rows, left_shared, right_rows, right_shared, row_table, col_table):
    left_split = left_rows.reshape((N_DP, TOK_DEV) + left_rows.shape[1:])
    right_split = right_rows.reshape((N_DP, TOK_DEV) + right_rows.shape[1:])
    per_replica = jax.vmap(lambda lhs, rhs: grads_ref(lhs, left_shared, rhs, right_shared, row_table, col_table))(left_split, right_split)
    return rounded(per_replica).sum(axis=0).astype(jnp.bfloat16)

def reference(tokens, gate_tiles, gate_index, gate_count, up_tiles, up_index, up_count, down_tiles, down_index, down_count, grad_output):
    gate_rt, gate_ct = tables_ref(gate_index, gate_count, D_OWN, F_OWN)
    up_rt, up_ct = tables_ref(up_index, up_count, D_OWN, F_OWN)
    down_rt, down_ct = tables_ref(down_index, down_count, F_OWN, D_OWN)
    gate_blocks = gate_tiles.reshape(N_MP, N_MP, CAP, TILE, TILE)
    up_blocks = up_tiles.reshape(N_MP, N_MP, CAP, TILE, TILE)
    down_blocks = down_tiles.reshape(N_MP, N_MP, CAP, TILE, TILE)
    token_groups = tokens.reshape(TOKENS, N_MP, D_OWN, TILE).transpose(1, 0, 2, 3)

    def hidden_step(total, inputs):
        rows_q, gate_q, gate_rq, gate_cq, up_q, up_rq, up_cq = inputs
        gate_term = forward_ref(rows_q, True, gate_q, gate_rq, gate_cq, False).reshape(TOKENS, FF)
        up_term = forward_ref(rows_q, True, up_q, up_rq, up_cq, False).reshape(TOKENS, FF)
        return ((total[0] + rounded(gate_term), total[1] + rounded(up_term)), None)
    zeros_hidden = jnp.zeros((TOKENS, FF), jnp.float32)
    (gate, up), _ = lax.scan(hidden_step, (zeros_hidden, zeros_hidden), (token_groups, gate_blocks, gate_rt, gate_ct, up_blocks, up_rt, up_ct))
    sigmoid_gate = jax.nn.sigmoid(gate)
    activated = gate * sigmoid_gate
    hidden = (activated * up).astype(jnp.bfloat16)
    hidden_groups = hidden.reshape(TOKENS, N_MP, F_OWN, TILE).transpose(1, 0, 2, 3)

    def output_step(total, inputs):
        rows_e, down_e, row_e, col_e = inputs
        term = forward_ref(rows_e, True, down_e, row_e, col_e, False).reshape(TOKENS, D)
        return (total + rounded(term), None)
    output_sum, _ = lax.scan(output_step, jnp.zeros((TOKENS, D), jnp.float32), (hidden_groups, down_blocks, down_rt, down_ct))
    layer_output = output_sum.astype(jnp.bfloat16)
    cotangent = grad_output.reshape(TOKENS, N_MP, D_OWN, TILE)

    def hidden_grad(inputs):
        down_e, row_e, col_e = inputs
        return backward_ref(cotangent, False, down_e, row_e, col_e, True)
    grad_hidden = lax.map(hidden_grad, (down_blocks, down_rt, down_ct)).transpose(1, 0, 2, 3).reshape(TOKENS, FF)
    grad_gate_pre = (grad_hidden * up * (sigmoid_gate * (1.0 + gate * (1.0 - sigmoid_gate)))).astype(jnp.bfloat16)
    grad_up_pre = (grad_hidden * activated).astype(jnp.bfloat16)
    gate_cols = grad_gate_pre.reshape(TOKENS, N_MP, F_OWN, TILE)
    up_cols = grad_up_pre.reshape(TOKENS, N_MP, F_OWN, TILE)

    def input_grad(inputs):
        gate_q, gate_rq, gate_cq, up_q, up_rq, up_cq = inputs
        contrib = backward_ref(gate_cols, False, gate_q, gate_rq, gate_cq, False)
        contrib = contrib + backward_ref(up_cols, False, up_q, up_rq, up_cq, False)
        return rounded(contrib).sum(axis=1)
    grad_parts = lax.map(input_grad, (gate_blocks, gate_rt, gate_ct, up_blocks, up_rt, up_ct))
    grad_tokens = grad_parts.transpose(1, 0, 2, 3).reshape(TOKENS, D).astype(jnp.bfloat16)

    def gate_tile_grad(inputs):
        rows_q, row_q, col_q = inputs
        return replica_sum(rows_q, True, gate_cols, False, row_q, col_q)

    def up_tile_grad(inputs):
        rows_q, row_q, col_q = inputs
        return replica_sum(rows_q, True, up_cols, False, row_q, col_q)

    def down_tile_grad(inputs):
        rows_e, row_e, col_e = inputs
        return replica_sum(rows_e, True, cotangent, False, row_e, col_e)
    flat_shape = (NTILES * TILE // 2, 2 * TILE)
    grad_gate = lax.map(gate_tile_grad, (token_groups, gate_rt, gate_ct)).reshape(flat_shape)
    grad_up = lax.map(up_tile_grad, (token_groups, up_rt, up_ct)).reshape(flat_shape)
    grad_down = lax.map(down_tile_grad, (hidden_groups, down_rt, down_ct)).reshape(flat_shape)
    return (layer_output, grad_tokens, grad_gate, grad_up, grad_down)
```

```python
import jax
import jax.numpy as jnp
from jax import lax
from jax.experimental import pallas as pl
from jax.experimental.pallas import tpu as pltpu
from jax.sharding import PartitionSpec as P

FF = 14336
TILE = 64
HALF = TILE // 2
DEPTH = 8
D_OWN = 8
F_OWN = 14
GROUPS = 16
SIDE = 4
CHUNKS = 4
BF = jnp.bfloat16
F32 = jnp.float32


def tn(a, b):
    return lax.dot_general(a, b, (((0,), (0,)), ((), ())), preferred_element_type=F32)


def nn(a, b):
    return lax.dot_general(a, b, (((1,), (0,)), ((), ())), preferred_element_type=F32)


def nt(a, b):
    return lax.dot_general(a, b, (((1,), (1,)), ((), ())), preferred_element_type=F32)


def unpack(tile):
    return jnp.concatenate([tile[:, :TILE], tile[:, TILE:]], axis=0)


def pack(values):
    return jnp.concatenate([values[:HALF], values[HALF:]], axis=1)


def down_kernel(dmeta, act, down, grad_hidden, down_t, cot, acc, sems):
    span = GROUPS // CHUNKS
    copies = [
        pltpu.make_async_copy(
            act.at[pl.ds(n * span, span), 1], cot.at[pl.ds(n * span, span)], sems.at[n]
        )
        for n in range(CHUNKS)
    ]
    for copy in copies:
        copy.start()
    for f in range(F_OWN):
        acc[f] = jnp.zeros((TILE, 128), F32)

    for n in range(CHUNKS):
        copies[n].wait()

        @pl.loop(n * span, (n + 1) * span, unroll=span)
        def _(e):
            tiles = [unpack(down[e * DEPTH + c]) for c in range(DEPTH)]
            parts = [nn(tiles[c], cot[e, dmeta[1, e * DEPTH + c]]) for c in range(DEPTH)]
            for c in range(DEPTH):
                acc[dmeta[0, e * DEPTH + c]] += parts[c]

    @pl.loop(0, GROUPS, unroll=2)
    def _(e):
        for c in range(DEPTH):
            down_t[e * DEPTH + c] = unpack(down[e * DEPTH + c]).T

    for f in range(F_OWN):
        grad_hidden[f, pl.ds(0, HALF, stride=2), :] = acc[f, :HALF]
        grad_hidden[f, pl.ds(1, HALF, stride=2), :] = acc[f, HALF:]


def layer_kernel(
    meta,
    dmeta,
    act,
    gu,
    grad_hidden,
    grads,
    hidden_split,
    pre,
    pairs,
    tiles,
    tokens,
    cot,
    grads_v,
    acc,
    strided,
    sems,
):
    span = GROUPS // CHUNKS

    def loads(n):
        rows = pl.ds(n * span, span)
        return (
            pltpu.make_async_copy(act.at[rows, 2], pairs.at[rows], sems.at[0, n]),
            pltpu.make_async_copy(gu.at[:, rows], tiles.at[:, rows], sems.at[1, n]),
        )

    first = [loads(n) for n in range(CHUNKS)]
    load_tokens = pltpu.make_async_copy(act.at[:, 0], tokens, sems.at[2, 0])
    load_cot = pltpu.make_async_copy(act.at[:, 1], cot, sems.at[2, 1])
    store = pltpu.make_async_copy(grads_v, grads, sems.at[2, 2])
    for pair in first:
        for copy in pair:
            copy.start()
    load_tokens.start()
    load_cot.start()
    for f in range(2 * F_OWN):
        acc[f] = jnp.zeros((128, TILE), F32)

    for n in range(CHUNKS):
        for copy in first[n]:
            copy.wait()

        @pl.loop(n * span, (n + 1) * span, unroll=span)
        def _(q):
            for base in range(0, 2 * DEPTH, 4):
                parts = []
                for m in range(base, base + 4):
                    tile = unpack(tiles[m, q])
                    row = meta[q, m]
                    odd = jnp.broadcast_to(row % 2, tile.shape) > 0
                    none = jnp.zeros_like(tile)
                    tall = jnp.concatenate(
                        [jnp.where(odd, none, tile), jnp.where(odd, tile, none)], axis=0
                    )
                    pair = 2 * (row // 2)
                    both = jnp.concatenate([pairs[q, pair], pairs[q, pair + 1]], axis=0)
                    parts.append(nn(both, tall))
                for m in range(base, base + 4):
                    acc[meta[q, 2 * DEPTH + m]] += parts[m - base]

    for f in range(F_OWN):
        back = grad_hidden[f]
        gate = acc[f].T
        up = acc[F_OWN + f].T
        sig = jax.nn.sigmoid(gate)
        activated = gate * sig
        pre[f] = (back * up * (sig * (1.0 + gate * (1.0 - sig)))).astype(BF)
        pre[F_OWN + f] = (back * activated).astype(BF)
        strided[f] = activated * up
        hidden_split[f, :HALF] = strided[f, pl.ds(0, HALF, stride=2), :].astype(BF)
        hidden_split[f, HALF:] = strided[f, pl.ds(1, HALF, stride=2), :].astype(BF)

    load_tokens.wait()

    @pl.loop(0, GROUPS, unroll=8)
    def _(q):
        for m in range(2 * DEPTH):
            got = nt(tokens[q, meta[q, m]], pre[meta[q, 2 * DEPTH + m]])
            grads_v[m, q] = pack(got.astype(BF))

    load_cot.wait()

    @pl.loop(0, GROUPS, unroll=8)
    def _(q):
        for c in range(DEPTH):
            k = q * DEPTH + c
            got = nt(hidden_split[dmeta[0, k]], cot[q, dmeta[1, k]])
            live = jnp.broadcast_to(dmeta[2, k], got.shape) > 0
            grads_v[q, GROUPS + c] = pack(jnp.where(live, got, 0.0).astype(BF))

    store.start()
    store.wait()


def output_kernel(meta, dmeta, gu, down_t, hidden_split, pre, partials, tiles, turned, sums, acc, sems):
    span = GROUPS // CHUNKS
    zero_block = jnp.zeros((TILE, 128), F32)

    def loads(n):
        rows = pl.ds(n * span, span)
        flat = pl.ds(n * span * DEPTH, span * DEPTH)
        return (
            pltpu.make_async_copy(gu.at[:, rows], tiles.at[:, rows], sems.at[0, n]),
            pltpu.make_async_copy(down_t.at[flat], turned.at[flat], sems.at[1, n]),
        )

    def store(n):
        rows = pl.ds(n * span, span)
        return pltpu.make_async_copy(sums.at[rows], partials.at[rows], sems.at[2, n])

    first = [loads(n) for n in range(CHUNKS)]
    for pair in first:
        for copy in pair:
            copy.start()

    for n in range(CHUNKS):
        for copy in first[n]:
            copy.wait()

        @pl.loop(n * span, (n + 1) * span, unroll=span)
        def _(q):
            for r in range(D_OWN):
                acc[0, r] = zero_block
                acc[1, r] = zero_block
            for base in range(0, DEPTH, 4):
                parts = []
                for c in range(base, base + 4):
                    k = q * DEPTH + c
                    parts.append(nn(turned[k], hidden_split[dmeta[0, k]]))
                for c in range(base, base + 4):
                    acc[0, dmeta[1, q * DEPTH + c]] += parts[c - base]
            for base in range(0, 2 * DEPTH, 4):
                parts = []
                for m in range(base, base + 4):
                    parts.append(nn(unpack(tiles[m, q]), pre[meta[q, 2 * DEPTH + m]]))
                for m in range(base, base + 4):
                    acc[1, meta[q, m]] += parts[m - base]
            for r in range(D_OWN):
                sums[q, 0, r] = acc[0, r].astype(BF)
                sums[q, 1, r] = acc[1, r].astype(BF)

        store(n).start()
    for n in range(CHUNKS):
        store(n).wait()


SMEM = pl.BlockSpec(memory_space=pltpu.SMEM)
VMEM = pl.BlockSpec(memory_space=pltpu.VMEM)
ANY = pl.BlockSpec(memory_space=pl.ANY)
LIMIT = 48 * 1024 * 1024


def down_part(dmeta, act, down):
    return pl.pallas_call(
        down_kernel,
        out_shape=(
            jax.ShapeDtypeStruct((F_OWN, TILE, 128), F32),
            jax.ShapeDtypeStruct((GROUPS * DEPTH, TILE, TILE), BF),
        ),
        in_specs=[SMEM, ANY, VMEM],
        out_specs=(VMEM, VMEM),
        scratch_shapes=[
            pltpu.VMEM((GROUPS, D_OWN, TILE, 128), BF),
            pltpu.VMEM((F_OWN, TILE, 128), F32),
            pltpu.SemaphoreType.DMA((CHUNKS,)),
        ],
        compiler_params=pltpu.CompilerParams(vmem_limit_bytes=LIMIT),
        cost_estimate=pl.CostEstimate(flops=2**27, bytes_accessed=2**23, transcendentals=0),
        name="down_kernel",
    )(dmeta, act, down)


def layer(meta, dmeta, act, gu, grad_hidden):
    block = (GROUPS, D_OWN, TILE, 128)
    return pl.pallas_call(
        layer_kernel,
        out_shape=(
            jax.ShapeDtypeStruct((GROUPS, 3 * DEPTH, HALF, 128), BF),
            jax.ShapeDtypeStruct((F_OWN, TILE, 128), BF),
            jax.ShapeDtypeStruct((2 * F_OWN, TILE, 128), BF),
        ),
        in_specs=[SMEM, SMEM, ANY, ANY, VMEM],
        out_specs=(ANY, VMEM, VMEM),
        scratch_shapes=[
            pltpu.VMEM(block, BF),
            pltpu.VMEM((2 * DEPTH, GROUPS, HALF, 128), BF),
            pltpu.VMEM(block, BF),
            pltpu.VMEM(block, BF),
            pltpu.VMEM((GROUPS, 3 * DEPTH, HALF, 128), BF),
            pltpu.VMEM((2 * F_OWN, 128, TILE), F32),
            pltpu.VMEM((F_OWN, TILE, 128), F32),
            pltpu.SemaphoreType.DMA((3, CHUNKS)),
        ],
        compiler_params=pltpu.CompilerParams(vmem_limit_bytes=LIMIT),
        cost_estimate=pl.CostEstimate(flops=2**29, bytes_accessed=2**23, transcendentals=0),
        name="layer_kernel",
    )(meta, dmeta, act, gu, grad_hidden)


def output_part(meta, dmeta, gu, down_t, hidden_split, pre):
    return pl.pallas_call(
        output_kernel,
        out_shape=jax.ShapeDtypeStruct((GROUPS, 2, D_OWN, TILE, 128), BF),
        in_specs=[SMEM, SMEM, ANY, ANY, VMEM, VMEM],
        out_specs=ANY,
        scratch_shapes=[
            pltpu.VMEM((2 * DEPTH, GROUPS, HALF, 128), BF),
            pltpu.VMEM((GROUPS * DEPTH, TILE, TILE), BF),
            pltpu.VMEM((GROUPS, 2, D_OWN, TILE, 128), BF),
            pltpu.VMEM((2, D_OWN, TILE, 128), F32),
            pltpu.SemaphoreType.DMA((3, CHUNKS)),
        ],
        compiler_params=pltpu.CompilerParams(vmem_limit_bytes=LIMIT),
        cost_estimate=pl.CostEstimate(flops=2**28, bytes_accessed=2**23, transcendentals=0),
        name="output_kernel",
    )(meta, dmeta, gu, down_t, hidden_split, pre)


def split_order(size):
    n = jnp.arange(size, dtype=jnp.int32)
    block, inner = n // TILE, n % TILE
    source = block * TILE + 2 * (inner % HALF) + inner // HALF
    return (source[:, None] == n[None, :]).astype(BF)


def lines(second):
    groups = []
    for mp in range(GROUPS):
        for other in range(SIDE):
            along_x = (mp % 2 == 0) != second
            groups.append(
                [
                    ((n * SIDE + other) if along_x else (other * SIDE + n)) * GROUPS + mp
                    for n in range(SIDE)
                ]
            )
    return groups


def exchange(parts, second):
    return lax.all_to_all(
        parts, ("dp", "mp"), 0, 0, tiled=True, axis_index_groups=lines(second)
    )


def spread(piece, second):
    return exchange(jnp.broadcast_to(piece[None], (SIDE,) + piece.shape), second)


def to_replicas(piece):
    got = spread(spread(piece, True), False)
    return got.reshape((GROUPS,) + piece.shape)


def from_replicas(parts):
    parts = parts.reshape((SIDE, SIDE) + parts.shape[1:])
    for second in (False, True):
        parts = exchange(parts, second).astype(F32).sum(axis=0).astype(BF)
    return parts


def per_device(
    tokens,
    gate_tiles,
    gate_index,
    gate_count,
    up_tiles,
    up_index,
    up_count,
    down_tiles,
    down_index,
    down_count,
    grad_output,
):
    me = lax.axis_index("mp")
    replica = lax.axis_index("dp")
    crossed = me % 2
    turned = (replica % SIDE) * SIDE + replica // SIDE
    part = jnp.where(crossed == 1, turned, replica)
    width = tokens.shape[1]
    order = split_order(width)
    eye = jnp.eye(width, dtype=BF)
    groups = jnp.arange(GROUPS, dtype=jnp.int32)[:, None]
    slots = jnp.arange(DEPTH, dtype=jnp.int32)[None, :]

    tokens_t = jnp.einsum("pi,ti->pt", order, tokens, preferred_element_type=F32).astype(BF)
    grad_t = jnp.einsum("pi,ti->pt", eye, grad_output, preferred_element_type=F32).astype(BF)
    tokens_p = jnp.einsum("ti,pi->tp", tokens, order, preferred_element_type=F32).astype(BF)
    tokens_p = tokens_p.reshape(128, width // 128, 128).transpose(1, 0, 2).reshape(width, 128)
    own = jnp.concatenate([tokens_t, grad_t, tokens_p], axis=0)
    own, gate_index, up_index, gate_tiles, up_tiles = lax.optimization_barrier(
        (own, gate_index, up_index, gate_tiles, up_tiles)
    )
    act = lax.all_gather(own, "mp", axis=0)
    act = act.reshape(GROUPS, 3, D_OWN, TILE, 128)

    def blocks(index):
        return index.reshape(GROUPS, DEPTH, 2)

    is_up = part // DEPTH
    depth = part % DEPTH
    gate_t = lax.dynamic_index_in_dim(
        gate_tiles.reshape(GROUPS, DEPTH, HALF, 128), depth, 1, keepdims=False
    )
    up_t = lax.dynamic_index_in_dim(
        up_tiles.reshape(GROUPS, DEPTH, HALF, 128), depth, 1, keepdims=False
    )
    count = jnp.where(is_up == 1, up_count, gate_count)
    my_live = (depth < count)[:, None, None]
    mine = jnp.where(my_live, jnp.where(is_up == 1, up_t, gate_t), 0)
    gate_b, up_b = blocks(gate_index), blocks(up_index)
    notes = jnp.concatenate(
        [
            gate_b[..., 0] - me * D_OWN,
            up_b[..., 0] - me * D_OWN,
            gate_b[..., 1] - groups * F_OWN,
            up_b[..., 1] - groups * F_OWN + F_OWN,
        ],
        axis=1,
    ).astype(BF)
    notes = jnp.pad(notes[:, None, :], ((0, 0), (0, 7), (0, 128 - 4 * DEPTH)))
    sent = lax.all_to_all(
        jnp.concatenate([mine, notes], axis=1), "mp", 0, 0, tiled=True
    )
    meta = sent[:, HALF, : 4 * DEPTH].astype(jnp.int32).reshape(GROUPS, 2, SIDE, SIDE)
    same = (groups % 2 == crossed)[..., None, None]
    meta = jnp.where(same, meta, meta.swapaxes(2, 3)).reshape(GROUPS, 4 * DEPTH)
    gu = to_replicas(sent[:, :HALF])

    down_b = blocks(down_index)
    down_live = slots < down_count[:, None]
    dmeta = jnp.stack(
        [
            (down_b[..., 0] - me * F_OWN).reshape(-1),
            (down_b[..., 1] - groups * D_OWN).reshape(-1),
            down_live.astype(jnp.int32).reshape(-1),
        ]
    )
    down = jnp.where(
        down_live.reshape(-1)[:, None, None], down_tiles.reshape(GROUPS * DEPTH, HALF, 128), 0
    )

    grad_hidden, down_t = down_part(dmeta, act, down)
    grads, hidden_split, pre = layer(meta, dmeta, act, gu, grad_hidden)
    partials = output_part(meta, dmeta, gu, down_t, hidden_split, pre)

    summed = lax.psum_scatter(
        partials.reshape(GROUPS * 2 * width, 128), "mp", scatter_dimension=0, tiled=True
    )
    layer_output = jnp.einsum(
        "pt,pi->ti", summed[:width], eye, preferred_element_type=F32
    ).astype(BF)
    grad_tokens = jnp.einsum(
        "pt,pi->ti", summed[width:], order, preferred_element_type=F32
    ).astype(BF)

    got = from_replicas(grads)
    back = lax.all_to_all(got[:GROUPS], "mp", 0, 0, tiled=True)
    piece = jnp.concatenate([jnp.where(my_live, back, 0), got[GROUPS:]], axis=0)
    full = to_replicas(piece)
    flat = (GROUPS * DEPTH * HALF, 128)
    grad_gate = full[:DEPTH, :GROUPS].transpose(1, 0, 2, 3).reshape(flat)
    grad_up = full[DEPTH:, :GROUPS].transpose(1, 0, 2, 3).reshape(flat)
    grad_down = full[:, GROUPS:].reshape(flat)
    return (layer_output, grad_tokens, grad_gate, grad_up, grad_down)


def solution(mesh):
    return jax.shard_map(
        per_device,
        mesh=mesh,
        in_specs=(
            P("dp", "mp"),
            P("mp", None),
            P("mp", None),
            P("mp"),
            P("mp", None),
            P("mp", None),
            P("mp"),
            P("mp", None),
            P("mp", None),
            P("mp"),
            P("dp", "mp"),
        ),
        out_specs=(P("dp", "mp"), P("dp", "mp"), P("mp", None), P("mp", None), P("mp", None)),
        check_vma=False,
    )
```

```python
import jax
import jax.numpy as jnp
from jax import lax
from jax.experimental import pallas as pl
from jax.experimental.pallas import tpu as pltpu
from jax.sharding import PartitionSpec as P

FF = 14336
TILE = 64
HALF = TILE // 2
DEPTH = 8
D_OWN = 8
F_OWN = 14
GROUPS = 16
SIDE = 4
CHUNKS = 4
BF = jnp.bfloat16
F32 = jnp.float32


def tn(a, b):
    return lax.dot_general(a, b, (((0,), (0,)), ((), ())), preferred_element_type=F32)


def nn(a, b):
    return lax.dot_general(a, b, (((1,), (0,)), ((), ())), preferred_element_type=F32)


def nt(a, b):
    return lax.dot_general(a, b, (((1,), (1,)), ((), ())), preferred_element_type=F32)


def unpack(tile):
    return jnp.concatenate([tile[:, :TILE], tile[:, TILE:]], axis=0)


def pack(values):
    return jnp.concatenate([values[:HALF], values[HALF:]], axis=1)


def turn_kernel(down, down_t, turned, sems):
    span = GROUPS * DEPTH // CHUNKS
    for n in range(CHUNKS):
        flat = pl.ds(n * span, span)

        @pl.loop(n * span, (n + 1) * span, step=2 * DEPTH)
        def _(base):
            for c in range(2 * DEPTH):
                turned[base + c] = unpack(down[base + c]).T

        pltpu.make_async_copy(turned.at[flat], down_t.at[flat], sems.at[n]).start()
    for n in range(CHUNKS):
        flat = pl.ds(n * span, span)
        pltpu.make_async_copy(turned.at[flat], down_t.at[flat], sems.at[n]).wait()


def pieces(place):
    first = [(place[0] + SIDE - k) & (SIDE - 1) for k in range(SIDE)]
    second = [(place[1] + SIDE - k) & (SIDE - 1) for k in range(SIDE)]
    return [SIDE * i + j for i in first for j in second]


def tile_loads(gu, tiles, sems, n):
    rows = pl.ds(n * (GROUPS // CHUNKS), GROUPS // CHUNKS)
    return [
        pltpu.make_async_copy(
            gu[k].at[:, rows], tiles.at[pl.ds(k * SIDE, SIDE), rows], sems.at[k, n]
        )
        for k in range(SIDE)
    ]


def layer_kernel(
    place,
    meta,
    dmeta,
    act,
    down,
    gu_0,
    gu_1,
    gu_2,
    gu_3,
    grads_0,
    grads_1,
    grads_2,
    grads_3,
    hidden_split,
    pre,
    pairs,
    tiles,
    tokens,
    cot,
    grads_v,
    acc,
    acc_dh,
    strided,
    tile_sems,
    sems,
):
    span = GROUPS // CHUNKS
    gu = (gu_0, gu_1, gu_2, gu_3)
    grads = (grads_0, grads_1, grads_2, grads_3)
    slot = pieces(place)

    def plane(n, which, target):
        rows = pl.ds(n * span, span)
        return pltpu.make_async_copy(act.at[rows, which], target.at[rows], sems.at[which, n])

    load_cot = [plane(n, 1, cot) for n in range(CHUNKS)]
    load_pairs = [plane(n, 2, pairs) for n in range(CHUNKS)]
    load_tiles = [tile_loads(gu, tiles, tile_sems, n) for n in range(CHUNKS)]
    load_tokens = pltpu.make_async_copy(act.at[:, 0], tokens, sems.at[0, 0])
    for copy in load_cot:
        copy.start()
    for n in range(CHUNKS):
        load_pairs[n].start()
        for copy in load_tiles[n]:
            copy.start()
    load_tokens.start()
    for f in range(F_OWN):
        acc_dh[f] = jnp.zeros((TILE, 128), F32)
        acc[f] = jnp.zeros((128, TILE), F32)
        acc[F_OWN + f] = jnp.zeros((128, TILE), F32)

    for n in range(CHUNKS):
        load_cot[n].wait()

        @pl.loop(n * span, (n + 1) * span, unroll=span)
        def _(e):
            parts = [
                nn(unpack(down[e * DEPTH + c]), cot[e, dmeta[1, e * DEPTH + c]])
                for c in range(DEPTH)
            ]
            for c in range(DEPTH):
                acc_dh[dmeta[0, e * DEPTH + c]] += parts[c]

    for n in range(CHUNKS):
        load_pairs[n].wait()
        for copy in load_tiles[n]:
            copy.wait()

        @pl.loop(n * span, (n + 1) * span, unroll=span)
        def _(q):
            for base in range(0, 2 * DEPTH, 4):
                parts = []
                for m in range(base, base + 4):
                    tile = unpack(tiles[m, q])
                    row = meta[q, slot[m]]
                    odd = jnp.broadcast_to(row % 2, tile.shape) > 0
                    none = jnp.zeros_like(tile)
                    tall = jnp.concatenate(
                        [jnp.where(odd, none, tile), jnp.where(odd, tile, none)], axis=0
                    )
                    pair = 2 * (row // 2)
                    both = jnp.concatenate([pairs[q, pair], pairs[q, pair + 1]], axis=0)
                    parts.append(nn(both, tall))
                for m in range(base, base + 4):
                    acc[meta[q, 2 * DEPTH + slot[m]]] += parts[m - base]

    for f in range(F_OWN):
        strided[f, pl.ds(0, HALF, stride=2), :] = acc_dh[f, :HALF]
        strided[f, pl.ds(1, HALF, stride=2), :] = acc_dh[f, HALF:]
    for f in range(F_OWN):
        back = strided[f]
        gate = acc[f].T
        up = acc[F_OWN + f].T
        sig = jax.nn.sigmoid(gate)
        activated = gate * sig
        pre[f] = (back * up * (sig * (1.0 + gate * (1.0 - sig)))).astype(BF)
        pre[F_OWN + f] = (back * activated).astype(BF)
        acc_dh[f] = activated * up
    for f in range(F_OWN):
        hidden_split[f, :HALF] = acc_dh[f, pl.ds(0, HALF, stride=2), :].astype(BF)
        hidden_split[f, HALF:] = acc_dh[f, pl.ds(1, HALF, stride=2), :].astype(BF)

    @pl.loop(0, GROUPS, unroll=8)
    def _(q):
        for c in range(DEPTH):
            k = q * DEPTH + c
            got = nt(hidden_split[dmeta[0, k]], cot[q, dmeta[1, k]])
            live = jnp.broadcast_to(dmeta[2, k], got.shape) > 0
            grads_v[q, GROUPS + c] = pack(jnp.where(live, got, 0.0).astype(BF))

    def stores(k, part, which):
        rows = pl.ds(SIDE * ((place[0] + k) & (SIDE - 1)), SIDE)
        return pltpu.make_async_copy(
            grads_v.at[rows, part], grads[k].at[:, part], sems.at[3 + which, k]
        )

    in_gu, in_down = pl.ds(0, GROUPS), pl.ds(GROUPS, DEPTH)
    for k in range(SIDE):
        stores(k, in_down, 0).start()
    load_tokens.wait()

    @pl.loop(0, GROUPS, unroll=8)
    def _(q):
        for m in range(2 * DEPTH):
            got = nt(tokens[q, meta[q, m]], pre[meta[q, 2 * DEPTH + m]])
            grads_v[m, q] = pack(got.astype(BF))

    for k in range(SIDE):
        stores(k, in_gu, 1).start()
    for k in range(SIDE):
        stores(k, in_down, 0).wait()
        stores(k, in_gu, 1).wait()


def output_kernel(
    place,
    meta,
    dmeta,
    down_t,
    hidden_split,
    pre,
    gu_0,
    gu_1,
    gu_2,
    gu_3,
    partials,
    tiles,
    turned,
    sums,
    acc,
    tile_sems,
    sems,
):
    span = GROUPS // CHUNKS
    slot = pieces(place)
    zero_block = jnp.zeros((TILE, 128), F32)

    def load_turned(n):
        flat = pl.ds(n * span * DEPTH, span * DEPTH)
        return pltpu.make_async_copy(down_t.at[flat], turned.at[flat], sems.at[0, n])

    def store(n):
        rows = pl.ds(n * span, span)
        return pltpu.make_async_copy(sums.at[rows], partials.at[rows], sems.at[1, n])

    load_tiles = [tile_loads((gu_0, gu_1, gu_2, gu_3), tiles, tile_sems, n) for n in range(CHUNKS)]
    for n in range(CHUNKS):
        load_turned(n).start()
        for copy in load_tiles[n]:
            copy.start()

    for n in range(CHUNKS):
        load_turned(n).wait()
        for copy in load_tiles[n]:
            copy.wait()

        @pl.loop(n * span, (n + 1) * span, unroll=span)
        def _(q):
            for r in range(D_OWN):
                acc[0, r] = zero_block
                acc[1, r] = zero_block
            for base in range(0, DEPTH, 4):
                parts = []
                for c in range(base, base + 4):
                    k = q * DEPTH + c
                    parts.append(nn(turned[k], hidden_split[dmeta[0, k]]))
                for c in range(base, base + 4):
                    acc[0, dmeta[1, q * DEPTH + c]] += parts[c - base]
            for base in range(0, 2 * DEPTH, 4):
                parts = []
                for m in range(base, base + 4):
                    parts.append(nn(unpack(tiles[m, q]), pre[meta[q, 2 * DEPTH + slot[m]]]))
                for m in range(base, base + 4):
                    acc[1, meta[q, slot[m]]] += parts[m - base]
            for r in range(D_OWN):
                sums[q, 0, r] = acc[0, r].astype(BF)
                sums[q, 1, r] = acc[1, r].astype(BF)

        store(n).start()
    for n in range(CHUNKS):
        store(n).wait()


def turn_back(summed, layer_output, grad_tokens, ordered):
    width = D_OWN * TILE
    for r in range(D_OWN):
        for odd in range(2):
            rows = summed[pl.ds(width + r * TILE + odd * HALF, HALF), :]
            ordered[pl.ds(r * TILE + odd, HALF, stride=2), :] = rows.astype(F32)
    for n in range(width // 128):
        lanes = pl.ds(n * 128, 128)
        layer_output[:, lanes] = summed[lanes, :].T
        grad_tokens[:, lanes] = ordered[lanes, :].T.astype(BF)


def finish_kernel(
    place,
    summed,
    full_0,
    full_1,
    full_2,
    full_3,
    layer_output,
    grad_tokens,
    gate,
    up,
    down,
    ordered,
    sems,
):
    full = (full_0, full_1, full_2, full_3)
    for phase in range(2):
        if phase == 1:
            turn_back(summed, layer_output, grad_tokens, ordered)
        for k in range(SIDE):
            first = (place[0] + SIDE - k) & (SIDE - 1)
            for j in range(SIDE):
                second = (place[1] + SIDE - j) & (SIDE - 1)
                slot = SIDE * k + j
                to_down = pltpu.make_async_copy(
                    full[k].at[j, pl.ds(GROUPS, DEPTH)], down.at[SIDE * first + second], sems.at[1, slot]
                )
                depth = SIDE * (first & 1) + second
                source = full[k].at[j, pl.ds(0, GROUPS)]
                to_gate = pltpu.make_async_copy(source, gate.at[:, depth], sems.at[0, slot])
                to_up = pltpu.make_async_copy(source, up.at[:, depth], sems.at[0, slot])
                for copy, when in ((to_gate, first < 2), (to_up, first >= 2)):

                    @pl.when(when)
                    def _(copy=copy):
                        if phase == 0:
                            copy.start()
                        else:
                            copy.wait()

                if phase == 0:
                    to_down.start()
                else:
                    to_down.wait()


SMEM = pl.BlockSpec(memory_space=pltpu.SMEM)
VMEM = pl.BlockSpec(memory_space=pltpu.VMEM)
ANY = pl.BlockSpec(memory_space=pl.ANY)
LIMIT = 48 * 1024 * 1024
SMALL = 16 * 1024 * 1024


def turn(down):
    whole = (GROUPS * DEPTH, TILE, TILE)
    return pl.pallas_call(
        turn_kernel,
        out_shape=jax.ShapeDtypeStruct(whole, BF),
        in_specs=[VMEM],
        out_specs=ANY,
        scratch_shapes=[pltpu.VMEM(whole, BF), pltpu.SemaphoreType.DMA((CHUNKS,))],
        compiler_params=pltpu.CompilerParams(vmem_limit_bytes=LIMIT),
        cost_estimate=pl.CostEstimate(flops=2**26, bytes_accessed=2**22, transcendentals=0),
        name="turn_kernel",
    )(down)


def layer(place, meta, dmeta, act, down, gu):
    block = (GROUPS, D_OWN, TILE, 128)
    piece = jax.ShapeDtypeStruct((SIDE, 3 * DEPTH, HALF, 128), BF)
    *grads, hidden_split, pre = pl.pallas_call(
        layer_kernel,
        out_shape=(piece,) * SIDE
        + (
            jax.ShapeDtypeStruct((F_OWN, TILE, 128), BF),
            jax.ShapeDtypeStruct((2 * F_OWN, TILE, 128), BF),
        ),
        in_specs=[SMEM, SMEM, SMEM, ANY, VMEM] + [ANY] * SIDE,
        out_specs=(ANY,) * SIDE + (VMEM, VMEM),
        scratch_shapes=[
            pltpu.VMEM(block, BF),
            pltpu.VMEM((2 * DEPTH, GROUPS, HALF, 128), BF),
            pltpu.VMEM(block, BF),
            pltpu.VMEM(block, BF),
            pltpu.VMEM((GROUPS, 3 * DEPTH, HALF, 128), BF),
            pltpu.VMEM((2 * F_OWN, 128, TILE), F32),
            pltpu.VMEM((F_OWN, TILE, 128), F32),
            pltpu.VMEM((F_OWN, TILE, 128), F32),
            pltpu.SemaphoreType.DMA((SIDE, CHUNKS)),
            pltpu.SemaphoreType.DMA((5, CHUNKS)),
        ],
        compiler_params=pltpu.CompilerParams(vmem_limit_bytes=LIMIT),
        cost_estimate=pl.CostEstimate(flops=2**29, bytes_accessed=2**23, transcendentals=0),
        name="layer_kernel",
    )(place, meta, dmeta, act, down, *gu)
    return grads, hidden_split, pre


def output_part(place, meta, dmeta, down_t, hidden_split, pre, gu):
    return pl.pallas_call(
        output_kernel,
        out_shape=jax.ShapeDtypeStruct((GROUPS, 2, D_OWN, TILE, 128), BF),
        in_specs=[SMEM, SMEM, SMEM, ANY, VMEM, VMEM] + [ANY] * SIDE,
        out_specs=ANY,
        scratch_shapes=[
            pltpu.VMEM((2 * DEPTH, GROUPS, HALF, 128), BF),
            pltpu.VMEM((GROUPS * DEPTH, TILE, TILE), BF),
            pltpu.VMEM((GROUPS, 2, D_OWN, TILE, 128), BF),
            pltpu.VMEM((2, D_OWN, TILE, 128), F32),
            pltpu.SemaphoreType.DMA((SIDE, CHUNKS)),
            pltpu.SemaphoreType.DMA((2, CHUNKS)),
        ],
        compiler_params=pltpu.CompilerParams(vmem_limit_bytes=LIMIT),
        cost_estimate=pl.CostEstimate(flops=2**28, bytes_accessed=2**23, transcendentals=0),
        name="output_kernel",
    )(place, meta, dmeta, down_t, hidden_split, pre, *gu)


def finish(place, summed, full):
    tiles = jax.ShapeDtypeStruct((GROUPS, DEPTH, HALF, 128), BF)
    width = D_OWN * TILE
    rows = jax.ShapeDtypeStruct((128, width), BF)
    return pl.pallas_call(
        finish_kernel,
        out_shape=(rows,) * 2 + (tiles,) * 3,
        in_specs=[SMEM, VMEM] + [ANY] * SIDE,
        out_specs=(VMEM,) * 2 + (ANY,) * 3,
        scratch_shapes=[pltpu.VMEM((width, 128), F32), pltpu.SemaphoreType.DMA((2, SIDE * SIDE))],
        compiler_params=pltpu.CompilerParams(vmem_limit_bytes=SMALL),
        cost_estimate=pl.CostEstimate(flops=0, bytes_accessed=2**22, transcendentals=0),
        name="finish_kernel",
    )(place, summed, *full)


def split_order(size):
    n = jnp.arange(size, dtype=jnp.int32)
    block, inner = n // TILE, n % TILE
    source = block * TILE + 2 * (inner % HALF) + inner // HALF
    return (source[:, None] == n[None, :]).astype(BF)


def lines(second):
    groups = []
    for mp in range(GROUPS):
        for other in range(SIDE):
            along_x = (mp % 2 == 0) != second
            groups.append(
                [
                    ((n * SIDE + other) if along_x else (other * SIDE + n)) * GROUPS + mp
                    for n in range(SIDE)
                ]
            )
    return groups


def shift(value, second, count):
    pairs = [
        (line[n], line[(n + count) % SIDE]) for line in lines(second) for n in range(SIDE)
    ]
    return lax.ppermute(value, ("dp", "mp"), pairs)


def to_replicas(piece):
    row = jnp.stack([piece] + [shift(piece, True, k) for k in range(1, SIDE)])
    return [row] + [shift(row, False, k) for k in range(1, SIDE)]


def from_replicas(parts, second):
    got = parts
    rows = sum(part.astype(F32) for part in got).astype(BF)
    ahead = [
        lax.dynamic_index_in_dim(rows, (second + k) % SIDE, 0, keepdims=False)
        for k in range(SIDE)
    ]
    got = [ahead[0]] + [shift(ahead[k], True, k) for k in range(1, SIDE)]
    return sum(part.astype(F32) for part in got).astype(BF)


def per_device(
    tokens,
    gate_tiles,
    gate_index,
    gate_count,
    up_tiles,
    up_index,
    up_count,
    down_tiles,
    down_index,
    down_count,
    grad_output,
):
    me = lax.axis_index("mp")
    replica = lax.axis_index("dp")
    crossed = me % 2
    turned = (replica % SIDE) * SIDE + replica // SIDE
    part = jnp.where(crossed == 1, turned, replica)
    place = jnp.stack([part // SIDE, part % SIDE]).astype(jnp.int32)
    width = tokens.shape[1]
    order = split_order(width)
    eye = jnp.eye(width, dtype=BF)
    groups = jnp.arange(GROUPS, dtype=jnp.int32)[:, None]
    slots = jnp.arange(DEPTH, dtype=jnp.int32)[None, :]

    tokens_t = jnp.einsum("pi,ti->pt", order, tokens, preferred_element_type=F32).astype(BF)
    grad_t = jnp.einsum("pi,ti->pt", eye, grad_output, preferred_element_type=F32).astype(BF)
    tokens_p = jnp.einsum("ti,pi->tp", tokens, order, preferred_element_type=F32).astype(BF)
    tokens_p = tokens_p.reshape(128, width // 128, 128).transpose(1, 0, 2).reshape(width, 128)
    own = jnp.concatenate([tokens_t, grad_t, tokens_p], axis=0)
    own, gate_index, up_index, gate_tiles, up_tiles = lax.optimization_barrier(
        (own, gate_index, up_index, gate_tiles, up_tiles)
    )
    act = lax.all_gather(own, "mp", axis=0)
    act = act.reshape(GROUPS, 3, D_OWN, TILE, 128)

    def blocks(index):
        return index.reshape(GROUPS, DEPTH, 2)

    is_up = part // DEPTH
    depth = part % DEPTH
    gate_t = lax.dynamic_index_in_dim(
        gate_tiles.reshape(GROUPS, DEPTH, HALF, 128), depth, 1, keepdims=False
    )
    up_t = lax.dynamic_index_in_dim(
        up_tiles.reshape(GROUPS, DEPTH, HALF, 128), depth, 1, keepdims=False
    )
    count = jnp.where(is_up == 1, up_count, gate_count)
    my_live = (depth < count)[:, None, None]
    mine = jnp.where(my_live, jnp.where(is_up == 1, up_t, gate_t), 0)
    gate_b, up_b = blocks(gate_index), blocks(up_index)
    notes = jnp.concatenate(
        [
            gate_b[..., 0] - me * D_OWN,
            up_b[..., 0] - me * D_OWN,
            gate_b[..., 1] - groups * F_OWN,
            up_b[..., 1] - groups * F_OWN + F_OWN,
        ],
        axis=1,
    ).astype(BF)
    notes = jnp.pad(notes[:, None, :], ((0, 0), (0, 7), (0, 128 - 4 * DEPTH)))
    sent = lax.all_to_all(
        jnp.concatenate([mine, notes], axis=1), "mp", 0, 0, tiled=True
    )
    meta = sent[:, HALF, : 4 * DEPTH].astype(jnp.int32).reshape(GROUPS, 2, SIDE, SIDE)
    same = (groups % 2 == crossed)[..., None, None]
    meta = jnp.where(same, meta, meta.swapaxes(2, 3)).reshape(GROUPS, 4 * DEPTH)
    gu = to_replicas(sent[:, :HALF])

    down_b = blocks(down_index)
    down_live = slots < down_count[:, None]
    dmeta = jnp.stack(
        [
            (down_b[..., 0] - me * F_OWN).reshape(-1),
            (down_b[..., 1] - groups * D_OWN).reshape(-1),
            down_live.astype(jnp.int32).reshape(-1),
        ]
    )
    down = jnp.where(
        down_live.reshape(-1)[:, None, None], down_tiles.reshape(GROUPS * DEPTH, HALF, 128), 0
    )

    down_t = turn(down)
    down, down_t = lax.optimization_barrier((down, down_t))
    grads, hidden_split, pre = layer(place, meta, dmeta, act, down, gu)
    grads = [grads[0]] + [shift(grads[k], False, k) for k in range(1, SIDE)]
    partials = output_part(place, meta, dmeta, down_t, hidden_split, pre, gu)
    *grads, partials = lax.optimization_barrier((*grads, partials))

    summed = lax.psum_scatter(
        partials.reshape(GROUPS * 2 * width, 128), "mp", scatter_dimension=0, tiled=True
    )

    got = from_replicas(grads, part % SIDE)
    back = lax.all_to_all(got[:GROUPS], "mp", 0, 0, tiled=True)
    piece = jnp.concatenate([jnp.where(my_live, back, 0), got[GROUPS:]], axis=0)
    flat = (GROUPS * DEPTH * HALF, 128)
    layer_output, grad_tokens, *tile_grads = finish(place, summed, to_replicas(piece))
    grad_gate, grad_up, grad_down = (g.reshape(flat) for g in tile_grads)
    return (layer_output, grad_tokens, grad_gate, grad_up, grad_down)


def solution(mesh):
    return jax.shard_map(
        per_device,
        mesh=mesh,
        in_specs=(
            P("dp", "mp"),
            P("mp", None),
            P("mp", None),
            P("mp"),
            P("mp", None),
            P("mp", None),
            P("mp"),
            P("mp", None),
            P("mp", None),
            P("mp"),
            P("dp", "mp"),
        ),
        out_specs=(P("dp", "mp"), P("dp", "mp"), P("mp", None), P("mp", None), P("mp", None)),
        check_vma=False,
    )
```

```python
import jax
import jax.numpy as jnp
from jax import lax
from jax.experimental import pallas as pl
from jax.experimental.pallas import tpu as pltpu
from jax.sharding import PartitionSpec as P

FF = 14336
TILE = 64
HALF = TILE // 2
DEPTH = 8
D_OWN = 8
F_OWN = 14
GROUPS = 16
SIDE = 4
CHUNKS = 4
BF = jnp.bfloat16
F32 = jnp.float32


def tn(a, b):
    return lax.dot_general(a, b, (((0,), (0,)), ((), ())), preferred_element_type=F32)


def nn(a, b):
    return lax.dot_general(a, b, (((1,), (0,)), ((), ())), preferred_element_type=F32)


def nt(a, b):
    return lax.dot_general(a, b, (((1,), (1,)), ((), ())), preferred_element_type=F32)


def unpack(tile):
    return jnp.concatenate([tile[:, :TILE], tile[:, TILE:]], axis=0)


def pack(values):
    return jnp.concatenate([values[:HALF], values[HALF:]], axis=1)


def turn_kernel(down, down_t, turned, sems):
    span = GROUPS * DEPTH // CHUNKS
    for n in range(CHUNKS):
        flat = pl.ds(n * span, span)

        @pl.loop(n * span, (n + 1) * span, step=2 * DEPTH)
        def _(base):
            for c in range(2 * DEPTH):
                turned[base + c] = unpack(down[base + c]).T

        pltpu.make_async_copy(turned.at[flat], down_t.at[flat], sems.at[n]).start()
    for n in range(CHUNKS):
        flat = pl.ds(n * span, span)
        pltpu.make_async_copy(turned.at[flat], down_t.at[flat], sems.at[n]).wait()


def pieces(place):
    first = [(place[0] + SIDE - k) & (SIDE - 1) for k in range(SIDE)]
    second = [(place[1] + SIDE - k) & (SIDE - 1) for k in range(SIDE)]
    return [SIDE * i + j for i in first for j in second]


def tile_loads(gu, tiles, sems, n):
    rows = pl.ds(n * (GROUPS // CHUNKS), GROUPS // CHUNKS)
    return [
        pltpu.make_async_copy(
            gu[k].at[:, rows], tiles.at[pl.ds(k * SIDE, SIDE), rows], sems.at[k, n]
        )
        for k in range(SIDE)
    ]


def layer_kernel(
    place,
    meta,
    dmeta,
    act,
    down,
    gu_0,
    gu_1,
    gu_2,
    gu_3,
    grads_0,
    grads_1,
    grads_2,
    grads_3,
    hidden_split,
    pre,
    pairs,
    tiles,
    tokens,
    cot,
    grads_v,
    acc,
    acc_dh,
    strided,
    tile_sems,
    sems,
):
    span = GROUPS // CHUNKS
    gu = (gu_0, gu_1, gu_2, gu_3)
    grads = (grads_0, grads_1, grads_2, grads_3)
    slot = pieces(place)

    def plane(n, which, target):
        rows = pl.ds(n * span, span)
        return pltpu.make_async_copy(act.at[rows, which], target.at[rows], sems.at[which, n])

    load_cot = [plane(n, 1, cot) for n in range(CHUNKS)]
    load_pairs = [plane(n, 2, pairs) for n in range(CHUNKS)]
    load_tiles = [tile_loads(gu, tiles, tile_sems, n) for n in range(CHUNKS)]
    load_tokens = pltpu.make_async_copy(act.at[:, 0], tokens, sems.at[0, 0])
    for copy in load_cot:
        copy.start()
    for n in range(CHUNKS):
        load_pairs[n].start()
        for copy in load_tiles[n]:
            copy.start()
    load_tokens.start()
    for f in range(F_OWN):
        acc_dh[f] = jnp.zeros((TILE, 128), F32)
        acc[f] = jnp.zeros((128, TILE), F32)
        acc[F_OWN + f] = jnp.zeros((128, TILE), F32)

    for n in range(CHUNKS):
        load_cot[n].wait()

        @pl.loop(n * span, (n + 1) * span, unroll=span)
        def _(e):
            parts = [
                nn(unpack(down[e * DEPTH + c]), cot[e, dmeta[1, e * DEPTH + c]])
                for c in range(DEPTH)
            ]
            for c in range(DEPTH):
                acc_dh[dmeta[0, e * DEPTH + c]] += parts[c]

    for n in range(CHUNKS):
        load_pairs[n].wait()
        for copy in load_tiles[n]:
            copy.wait()

        @pl.loop(n * span, (n + 1) * span, unroll=span)
        def _(q):
            for base in range(0, 2 * DEPTH, 4):
                parts = []
                for m in range(base, base + 4):
                    tile = unpack(tiles[m, q])
                    row = meta[q, slot[m]]
                    odd = jnp.broadcast_to(row % 2, tile.shape) > 0
                    none = jnp.zeros_like(tile)
                    tall = jnp.concatenate(
                        [jnp.where(odd, none, tile), jnp.where(odd, tile, none)], axis=0
                    )
                    pair = 2 * (row // 2)
                    both = jnp.concatenate([pairs[q, pair], pairs[q, pair + 1]], axis=0)
                    parts.append(nn(both, tall))
                for m in range(base, base + 4):
                    acc[meta[q, 2 * DEPTH + slot[m]]] += parts[m - base]

    for f in range(F_OWN):
        strided[f, pl.ds(0, HALF, stride=2), :] = acc_dh[f, :HALF]
        strided[f, pl.ds(1, HALF, stride=2), :] = acc_dh[f, HALF:]
    for f in range(F_OWN):
        back = strided[f]
        gate = acc[f].T
        up = acc[F_OWN + f].T
        sig = jax.nn.sigmoid(gate)
        activated = gate * sig
        pre[f] = (back * up * (sig * (1.0 + gate * (1.0 - sig)))).astype(BF)
        pre[F_OWN + f] = (back * activated).astype(BF)
        acc_dh[f] = activated * up
    for f in range(F_OWN):
        hidden_split[f, :HALF] = acc_dh[f, pl.ds(0, HALF, stride=2), :].astype(BF)
        hidden_split[f, HALF:] = acc_dh[f, pl.ds(1, HALF, stride=2), :].astype(BF)

    @pl.loop(0, GROUPS, unroll=8)
    def _(q):
        for c in range(DEPTH):
            k = q * DEPTH + c
            got = nt(hidden_split[dmeta[0, k]], cot[q, dmeta[1, k]])
            live = jnp.broadcast_to(dmeta[2, k], got.shape) > 0
            grads_v[q, GROUPS + c] = pack(jnp.where(live, got, 0.0).astype(BF))

    def stores(k, part, which):
        rows = pl.ds(SIDE * ((place[0] + k) & (SIDE - 1)), SIDE)
        return pltpu.make_async_copy(
            grads_v.at[rows, part], grads[k].at[:, part], sems.at[3 + which, k]
        )

    in_gu, in_down = pl.ds(0, GROUPS), pl.ds(GROUPS, DEPTH)
    for k in range(SIDE):
        stores(k, in_down, 0).start()
    load_tokens.wait()

    @pl.loop(0, GROUPS, unroll=8)
    def _(q):
        for m in range(2 * DEPTH):
            got = nt(tokens[q, meta[q, m]], pre[meta[q, 2 * DEPTH + m]])
            grads_v[m, q] = pack(got.astype(BF))

    for k in range(SIDE):
        stores(k, in_gu, 1).start()
    for k in range(SIDE):
        stores(k, in_down, 0).wait()
        stores(k, in_gu, 1).wait()


def output_kernel(
    place,
    meta,
    dmeta,
    down_t,
    hidden_split,
    pre,
    gu_0,
    gu_1,
    gu_2,
    gu_3,
    partials,
    tiles,
    turned,
    sums,
    acc,
    tile_sems,
    sems,
):
    span = GROUPS // CHUNKS
    slot = pieces(place)
    zero_block = jnp.zeros((TILE, 128), F32)

    def load_turned(n):
        flat = pl.ds(n * span * DEPTH, span * DEPTH)
        return pltpu.make_async_copy(down_t.at[flat], turned.at[flat], sems.at[0, n])

    def store(n):
        rows = pl.ds(n * span, span)
        return pltpu.make_async_copy(sums.at[rows], partials.at[rows], sems.at[1, n])

    load_tiles = [tile_loads((gu_0, gu_1, gu_2, gu_3), tiles, tile_sems, n) for n in range(CHUNKS)]
    for n in range(CHUNKS):
        load_turned(n).start()
        for copy in load_tiles[n]:
            copy.start()

    for n in range(CHUNKS):
        load_turned(n).wait()
        for copy in load_tiles[n]:
            copy.wait()

        @pl.loop(n * span, (n + 1) * span, unroll=span)
        def _(q):
            for r in range(D_OWN):
                acc[0, r] = zero_block
                acc[1, r] = zero_block
            for base in range(0, DEPTH, 4):
                parts = []
                for c in range(base, base + 4):
                    k = q * DEPTH + c
                    parts.append(nn(turned[k], hidden_split[dmeta[0, k]]))
                for c in range(base, base + 4):
                    acc[0, dmeta[1, q * DEPTH + c]] += parts[c - base]
            for base in range(0, 2 * DEPTH, 4):
                parts = []
                for m in range(base, base + 4):
                    parts.append(nn(unpack(tiles[m, q]), pre[meta[q, 2 * DEPTH + slot[m]]]))
                for m in range(base, base + 4):
                    acc[1, meta[q, slot[m]]] += parts[m - base]
            for r in range(D_OWN):
                sums[q, 0, r] = acc[0, r].astype(BF)
                sums[q, 1, r] = acc[1, r].astype(BF)

        store(n).start()
    for n in range(CHUNKS):
        store(n).wait()


def turn_back_kernel(summed, layer_output, grad_tokens, held, ordered, sems):
    width = D_OWN * TILE

    def load(half):
        rows = pl.ds(half * width, width)
        return pltpu.make_async_copy(summed.at[rows], held.at[rows], sems.at[half])

    load(1).start()
    load(0).start()
    load(1).wait()
    for r in range(D_OWN):
        for odd in range(2):
            rows = held[pl.ds(width + r * TILE + odd * HALF, HALF), :]
            ordered[pl.ds(r * TILE + odd, HALF, stride=2), :] = rows.astype(F32)
    for n in range(width // 128):
        lanes = pl.ds(n * 128, 128)
        grad_tokens[:, lanes] = ordered[lanes, :].T.astype(BF)
    load(0).wait()
    for n in range(width // 128):
        lanes = pl.ds(n * 128, 128)
        layer_output[:, lanes] = held[lanes, :].T


def place_kernel(place, full_0, full_1, full_2, full_3, gate, up, down, sems):
    full = (full_0, full_1, full_2, full_3)
    for phase in range(2):
        for k in range(SIDE):
            first = (place[0] + SIDE - k) & (SIDE - 1)
            for j in range(SIDE):
                second = (place[1] + SIDE - j) & (SIDE - 1)
                slot = SIDE * k + j
                to_down = pltpu.make_async_copy(
                    full[k].at[j, pl.ds(GROUPS, DEPTH)], down.at[SIDE * first + second], sems.at[1, slot]
                )
                depth = SIDE * (first & 1) + second
                source = full[k].at[j, pl.ds(0, GROUPS)]
                to_gate = pltpu.make_async_copy(source, gate.at[:, depth], sems.at[0, slot])
                to_up = pltpu.make_async_copy(source, up.at[:, depth], sems.at[0, slot])
                for copy, when in ((to_gate, first < 2), (to_up, first >= 2)):

                    @pl.when(when)
                    def _(copy=copy):
                        if phase == 0:
                            copy.start()
                        else:
                            copy.wait()

                if phase == 0:
                    to_down.start()
                else:
                    to_down.wait()


SMEM = pl.BlockSpec(memory_space=pltpu.SMEM)
VMEM = pl.BlockSpec(memory_space=pltpu.VMEM)
ANY = pl.BlockSpec(memory_space=pl.ANY)
LIMIT = 48 * 1024 * 1024
SMALL = 16 * 1024 * 1024


def turn(down):
    whole = (GROUPS * DEPTH, TILE, TILE)
    return pl.pallas_call(
        turn_kernel,
        out_shape=jax.ShapeDtypeStruct(whole, BF),
        in_specs=[VMEM],
        out_specs=ANY,
        scratch_shapes=[pltpu.VMEM(whole, BF), pltpu.SemaphoreType.DMA((CHUNKS,))],
        compiler_params=pltpu.CompilerParams(vmem_limit_bytes=LIMIT),
        cost_estimate=pl.CostEstimate(flops=2**26, bytes_accessed=2**22, transcendentals=0),
        name="turn_kernel",
    )(down)


def layer(place, meta, dmeta, act, down, gu):
    block = (GROUPS, D_OWN, TILE, 128)
    piece = jax.ShapeDtypeStruct((SIDE, 3 * DEPTH, HALF, 128), BF)
    *grads, hidden_split, pre = pl.pallas_call(
        layer_kernel,
        out_shape=(piece,) * SIDE
        + (
            jax.ShapeDtypeStruct((F_OWN, TILE, 128), BF),
            jax.ShapeDtypeStruct((2 * F_OWN, TILE, 128), BF),
        ),
        in_specs=[SMEM, SMEM, SMEM, ANY, VMEM] + [ANY] * SIDE,
        out_specs=(ANY,) * SIDE + (VMEM, VMEM),
        scratch_shapes=[
            pltpu.VMEM(block, BF),
            pltpu.VMEM((2 * DEPTH, GROUPS, HALF, 128), BF),
            pltpu.VMEM(block, BF),
            pltpu.VMEM(block, BF),
            pltpu.VMEM((GROUPS, 3 * DEPTH, HALF, 128), BF),
            pltpu.VMEM((2 * F_OWN, 128, TILE), F32),
            pltpu.VMEM((F_OWN, TILE, 128), F32),
            pltpu.VMEM((F_OWN, TILE, 128), F32),
            pltpu.SemaphoreType.DMA((SIDE, CHUNKS)),
            pltpu.SemaphoreType.DMA((5, CHUNKS)),
        ],
        compiler_params=pltpu.CompilerParams(vmem_limit_bytes=LIMIT),
        cost_estimate=pl.CostEstimate(flops=2**29, bytes_accessed=2**23, transcendentals=0),
        name="layer_kernel",
    )(place, meta, dmeta, act, down, *gu)
    return grads, hidden_split, pre


def output_part(place, meta, dmeta, down_t, hidden_split, pre, gu):
    return pl.pallas_call(
        output_kernel,
        out_shape=jax.ShapeDtypeStruct((GROUPS, 2, D_OWN, TILE, 128), BF),
        in_specs=[SMEM, SMEM, SMEM, ANY, VMEM, VMEM] + [ANY] * SIDE,
        out_specs=ANY,
        scratch_shapes=[
            pltpu.VMEM((2 * DEPTH, GROUPS, HALF, 128), BF),
            pltpu.VMEM((GROUPS * DEPTH, TILE, TILE), BF),
            pltpu.VMEM((GROUPS, 2, D_OWN, TILE, 128), BF),
            pltpu.VMEM((2, D_OWN, TILE, 128), F32),
            pltpu.SemaphoreType.DMA((SIDE, CHUNKS)),
            pltpu.SemaphoreType.DMA((2, CHUNKS)),
        ],
        compiler_params=pltpu.CompilerParams(vmem_limit_bytes=LIMIT),
        cost_estimate=pl.CostEstimate(flops=2**28, bytes_accessed=2**23, transcendentals=0),
        name="output_kernel",
    )(place, meta, dmeta, down_t, hidden_split, pre, *gu)


def place_grads(place, full):
    tiles = jax.ShapeDtypeStruct((GROUPS, DEPTH, HALF, 128), BF)
    return pl.pallas_call(
        place_kernel,
        out_shape=(tiles,) * 3,
        in_specs=[SMEM] + [ANY] * SIDE,
        out_specs=(ANY,) * 3,
        scratch_shapes=[pltpu.SemaphoreType.DMA((2, SIDE * SIDE))],
        compiler_params=pltpu.CompilerParams(vmem_limit_bytes=SMALL),
        cost_estimate=pl.CostEstimate(flops=0, bytes_accessed=2**22, transcendentals=0),
        name="place_kernel",
    )(place, *full)


def turn_back(summed):
    width = D_OWN * TILE
    rows = jax.ShapeDtypeStruct((128, width), BF)
    return pl.pallas_call(
        turn_back_kernel,
        out_shape=(rows,) * 2,
        in_specs=[ANY],
        out_specs=(VMEM,) * 2,
        scratch_shapes=[
            pltpu.VMEM((2 * width, 128), BF),
            pltpu.VMEM((width, 128), F32),
            pltpu.SemaphoreType.DMA((2,)),
        ],
        compiler_params=pltpu.CompilerParams(vmem_limit_bytes=60 * 1024 * 1024),
        cost_estimate=pl.CostEstimate(flops=0, bytes_accessed=2**19, transcendentals=0),
        name="turn_back_kernel",
    )(summed)


def split_order(size):
    n = jnp.arange(size, dtype=jnp.int32)
    block, inner = n // TILE, n % TILE
    source = block * TILE + 2 * (inner % HALF) + inner // HALF
    return (source[:, None] == n[None, :]).astype(BF)


def lines(second):
    groups = []
    for mp in range(GROUPS):
        for other in range(SIDE):
            along_x = (mp % 2 == 0) != second
            groups.append(
                [
                    ((n * SIDE + other) if along_x else (other * SIDE + n)) * GROUPS + mp
                    for n in range(SIDE)
                ]
            )
    return groups


def shift(value, second, count):
    pairs = [
        (line[n], line[(n + count) % SIDE]) for line in lines(second) for n in range(SIDE)
    ]
    return lax.ppermute(value, ("dp", "mp"), pairs)


def to_replicas(piece):
    row = jnp.stack([piece] + [shift(piece, True, k) for k in range(1, SIDE)])
    return [row] + [shift(row, False, k) for k in range(1, SIDE)]


def from_replicas(parts, second):
    got = parts
    rows = sum(part.astype(F32) for part in got).astype(BF)
    ahead = [
        lax.dynamic_index_in_dim(rows, (second + k) % SIDE, 0, keepdims=False)
        for k in range(SIDE)
    ]
    got = [ahead[0]] + [shift(ahead[k], True, k) for k in range(1, SIDE)]
    return [
        sum(part[rows].astype(F32) for part in got).astype(BF)
        for rows in (slice(0, GROUPS), slice(GROUPS, None))
    ]


def per_device(
    tokens,
    gate_tiles,
    gate_index,
    gate_count,
    up_tiles,
    up_index,
    up_count,
    down_tiles,
    down_index,
    down_count,
    grad_output,
):
    me = lax.axis_index("mp")
    replica = lax.axis_index("dp")
    crossed = me % 2
    turned = (replica % SIDE) * SIDE + replica // SIDE
    part = jnp.where(crossed == 1, turned, replica)
    place = jnp.stack([part // SIDE, part % SIDE]).astype(jnp.int32)
    width = tokens.shape[1]
    order = split_order(width)
    eye = jnp.eye(width, dtype=BF)
    groups = jnp.arange(GROUPS, dtype=jnp.int32)[:, None]
    slots = jnp.arange(DEPTH, dtype=jnp.int32)[None, :]

    tokens_t = jnp.einsum("pi,ti->pt", order, tokens, preferred_element_type=F32).astype(BF)
    grad_t = jnp.einsum("pi,ti->pt", eye, grad_output, preferred_element_type=F32).astype(BF)
    tokens_p = jnp.einsum("ti,pi->tp", tokens, order, preferred_element_type=F32).astype(BF)
    tokens_p = tokens_p.reshape(128, width // 128, 128).transpose(1, 0, 2).reshape(width, 128)
    own = jnp.concatenate([tokens_t, grad_t, tokens_p], axis=0)
    own, gate_index, up_index, gate_tiles, up_tiles = lax.optimization_barrier(
        (own, gate_index, up_index, gate_tiles, up_tiles)
    )
    act = lax.all_gather(own, "mp", axis=0)
    act = act.reshape(GROUPS, 3, D_OWN, TILE, 128)

    def blocks(index):
        return index.reshape(GROUPS, DEPTH, 2)

    is_up = part // DEPTH
    depth = part % DEPTH
    gate_t = lax.dynamic_index_in_dim(
        gate_tiles.reshape(GROUPS, DEPTH, HALF, 128), depth, 1, keepdims=False
    )
    up_t = lax.dynamic_index_in_dim(
        up_tiles.reshape(GROUPS, DEPTH, HALF, 128), depth, 1, keepdims=False
    )
    count = jnp.where(is_up == 1, up_count, gate_count)
    my_live = (depth < count)[:, None, None]
    mine = jnp.where(my_live, jnp.where(is_up == 1, up_t, gate_t), 0)
    gate_b, up_b = blocks(gate_index), blocks(up_index)
    notes = jnp.concatenate(
        [
            gate_b[..., 0] - me * D_OWN,
            up_b[..., 0] - me * D_OWN,
            gate_b[..., 1] - groups * F_OWN,
            up_b[..., 1] - groups * F_OWN + F_OWN,
        ],
        axis=1,
    ).astype(BF)
    notes = jnp.pad(notes[:, None, :], ((0, 0), (0, 7), (0, 128 - 4 * DEPTH)))
    sent = lax.all_to_all(
        jnp.concatenate([mine, notes], axis=1), "mp", 0, 0, tiled=True
    )
    meta = sent[:, HALF, : 4 * DEPTH].astype(jnp.int32).reshape(GROUPS, 2, SIDE, SIDE)
    same = (groups % 2 == crossed)[..., None, None]
    meta = jnp.where(same, meta, meta.swapaxes(2, 3)).reshape(GROUPS, 4 * DEPTH)
    gu = to_replicas(sent[:, :HALF])

    down_b = blocks(down_index)
    down_live = slots < down_count[:, None]
    dmeta = jnp.stack(
        [
            (down_b[..., 0] - me * F_OWN).reshape(-1),
            (down_b[..., 1] - groups * D_OWN).reshape(-1),
            down_live.astype(jnp.int32).reshape(-1),
        ]
    )
    down = jnp.where(
        down_live.reshape(-1)[:, None, None], down_tiles.reshape(GROUPS * DEPTH, HALF, 128), 0
    )

    down_t = turn(down)
    down, down_t = lax.optimization_barrier((down, down_t))
    grads, hidden_split, pre = layer(place, meta, dmeta, act, down, gu)
    grads = [grads[0]] + [shift(grads[k], False, k) for k in range(1, SIDE)]
    partials = output_part(place, meta, dmeta, down_t, hidden_split, pre, gu)
    *grads, partials = lax.optimization_barrier((*grads, partials))

    summed = lax.psum_scatter(
        partials.reshape(GROUPS * 2 * width, 128), "mp", scatter_dimension=0, tiled=True
    )

    got_gu, got_down = from_replicas(grads, part % SIDE)
    back = lax.all_to_all(got_gu, "mp", 0, 0, tiled=True)
    piece = jnp.concatenate([jnp.where(my_live, back, 0), got_down], axis=0)
    flat = (GROUPS * DEPTH * HALF, 128)
    tile_grads = place_grads(place, to_replicas(piece))
    layer_output, grad_tokens = turn_back(summed)
    grad_gate, grad_up, grad_down = (g.reshape(flat) for g in tile_grads)
    return (layer_output, grad_tokens, grad_gate, grad_up, grad_down)


def solution(mesh):
    return jax.shard_map(
        per_device,
        mesh=mesh,
        in_specs=(
            P("dp", "mp"),
            P("mp", None),
            P("mp", None),
            P("mp"),
            P("mp", None),
            P("mp", None),
            P("mp"),
            P("mp", None),
            P("mp", None),
            P("mp"),
            P("dp", "mp"),
        ),
        out_specs=(P("dp", "mp"), P("dp", "mp"), P("mp", None), P("mp", None), P("mp", None)),
        check_vma=False,
    )
```

```python
import jax
import jax.numpy as jnp
from jax import lax
from jax.experimental import pallas as pl
from jax.experimental.pallas import tpu as pltpu
from jax.sharding import PartitionSpec as P

FF = 14336
TILE = 64
HALF = TILE // 2
DEPTH = 8
D_OWN = 8
F_OWN = 14
GROUPS = 16
SIDE = 4
CHUNKS = 4
BF = jnp.bfloat16
F32 = jnp.float32


def tn(a, b):
    return lax.dot_general(a, b, (((0,), (0,)), ((), ())), preferred_element_type=F32)


def nn(a, b):
    return lax.dot_general(a, b, (((1,), (0,)), ((), ())), preferred_element_type=F32)


def nt(a, b):
    return lax.dot_general(a, b, (((1,), (1,)), ((), ())), preferred_element_type=F32)


def unpack(tile):
    return jnp.concatenate([tile[:, :TILE], tile[:, TILE:]], axis=0)


def pack(values):
    return jnp.concatenate([values[:HALF], values[HALF:]], axis=1)


def turn_kernel(down, down_t, turned, sems):
    span = GROUPS * DEPTH // CHUNKS
    for n in range(CHUNKS):
        flat = pl.ds(n * span, span)

        @pl.loop(n * span, (n + 1) * span, step=2 * DEPTH)
        def _(base):
            for c in range(2 * DEPTH):
                turned[base + c] = unpack(down[base + c]).T

        pltpu.make_async_copy(turned.at[flat], down_t.at[flat], sems.at[n]).start()
    for n in range(CHUNKS):
        flat = pl.ds(n * span, span)
        pltpu.make_async_copy(turned.at[flat], down_t.at[flat], sems.at[n]).wait()


def pieces(place):
    first = [(place[0] + SIDE - k) & (SIDE - 1) for k in range(SIDE)]
    second = [(place[1] + SIDE - k) & (SIDE - 1) for k in range(SIDE)]
    return [SIDE * i + j for i in first for j in second]


def tile_loads(gu, tiles, sems, n):
    rows = pl.ds(n * (GROUPS // CHUNKS), GROUPS // CHUNKS)
    return [
        pltpu.make_async_copy(
            gu[k].at[:, rows], tiles.at[pl.ds(k * SIDE, SIDE), rows], sems.at[k, n]
        )
        for k in range(SIDE)
    ]


def layer_kernel(
    place,
    meta,
    dmeta,
    act,
    down,
    gu_0,
    gu_1,
    gu_2,
    gu_3,
    grads_0,
    grads_1,
    grads_2,
    grads_3,
    hidden_split,
    pre,
    pairs,
    tiles,
    tokens,
    cot,
    grads_v,
    acc,
    acc_dh,
    strided,
    tile_sems,
    sems,
):
    span = GROUPS // CHUNKS
    gu = (gu_0, gu_1, gu_2, gu_3)
    grads = (grads_0, grads_1, grads_2, grads_3)
    slot = pieces(place)

    def plane(n, which, target):
        rows = pl.ds(n * span, span)
        return pltpu.make_async_copy(act.at[rows, which], target.at[rows], sems.at[which, n])

    load_cot = [plane(n, 1, cot) for n in range(CHUNKS)]
    load_pairs = [plane(n, 2, pairs) for n in range(CHUNKS)]
    load_tiles = [tile_loads(gu, tiles, tile_sems, n) for n in range(CHUNKS)]
    load_tokens = pltpu.make_async_copy(act.at[:, 0], tokens, sems.at[0, 0])
    for copy in load_cot:
        copy.start()
    for n in range(CHUNKS):
        load_pairs[n].start()
        for copy in load_tiles[n]:
            copy.start()
    load_tokens.start()
    for f in range(F_OWN):
        acc_dh[f] = jnp.zeros((TILE, 128), F32)
        acc[f] = jnp.zeros((128, TILE), F32)
        acc[F_OWN + f] = jnp.zeros((128, TILE), F32)

    for n in range(CHUNKS):
        load_cot[n].wait()

        @pl.loop(n * span, (n + 1) * span, unroll=span)
        def _(e):
            parts = [
                nn(unpack(down[e * DEPTH + c]), cot[e, dmeta[1, e * DEPTH + c]])
                for c in range(DEPTH)
            ]
            for c in range(DEPTH):
                acc_dh[dmeta[0, e * DEPTH + c]] += parts[c]

    for n in range(CHUNKS):
        load_pairs[n].wait()
        for copy in load_tiles[n]:
            copy.wait()

        @pl.loop(n * span, (n + 1) * span, unroll=span)
        def _(q):
            for base in range(0, 2 * DEPTH, 4):
                parts = []
                for m in range(base, base + 4):
                    tile = unpack(tiles[m, q])
                    row = meta[q, slot[m]]
                    odd = jnp.broadcast_to(row % 2, tile.shape) > 0
                    none = jnp.zeros_like(tile)
                    tall = jnp.concatenate(
                        [jnp.where(odd, none, tile), jnp.where(odd, tile, none)], axis=0
                    )
                    pair = 2 * (row // 2)
                    both = jnp.concatenate([pairs[q, pair], pairs[q, pair + 1]], axis=0)
                    parts.append(nn(both, tall))
                for m in range(base, base + 4):
                    acc[meta[q, 2 * DEPTH + slot[m]]] += parts[m - base]

    for f in range(F_OWN):
        strided[f, pl.ds(0, HALF, stride=2), :] = acc_dh[f, :HALF]
        strided[f, pl.ds(1, HALF, stride=2), :] = acc_dh[f, HALF:]
    for f in range(F_OWN):
        back = strided[f]
        gate = acc[f].T
        up = acc[F_OWN + f].T
        sig = jax.nn.sigmoid(gate)
        activated = gate * sig
        pre[f] = (back * up * (sig * (1.0 + gate * (1.0 - sig)))).astype(BF)
        pre[F_OWN + f] = (back * activated).astype(BF)
        acc_dh[f] = activated * up
    for f in range(F_OWN):
        hidden_split[f, :HALF] = acc_dh[f, pl.ds(0, HALF, stride=2), :].astype(BF)
        hidden_split[f, HALF:] = acc_dh[f, pl.ds(1, HALF, stride=2), :].astype(BF)

    @pl.loop(0, GROUPS, unroll=8)
    def _(q):
        for c in range(DEPTH):
            k = q * DEPTH + c
            got = nt(hidden_split[dmeta[0, k]], cot[q, dmeta[1, k]])
            live = jnp.broadcast_to(dmeta[2, k], got.shape) > 0
            grads_v[q, GROUPS + c] = pack(jnp.where(live, got, 0.0).astype(BF))

    def stores(k, part, which):
        rows = pl.ds(SIDE * ((place[0] + k) & (SIDE - 1)), SIDE)
        return pltpu.make_async_copy(
            grads_v.at[rows, part], grads[k].at[:, part], sems.at[3 + which, k]
        )

    in_gu, in_down = pl.ds(0, GROUPS), pl.ds(GROUPS, DEPTH)
    for k in range(SIDE):
        stores(k, in_down, 0).start()
    load_tokens.wait()

    @pl.loop(0, GROUPS, unroll=8)
    def _(q):
        for m in range(2 * DEPTH):
            got = nt(tokens[q, meta[q, m]], pre[meta[q, 2 * DEPTH + m]])
            grads_v[m, q] = pack(got.astype(BF))

    for k in range(SIDE):
        stores(k, in_gu, 1).start()
    for k in range(SIDE):
        stores(k, in_down, 0).wait()
        stores(k, in_gu, 1).wait()


def output_kernel(
    place,
    meta,
    dmeta,
    down_t,
    hidden_split,
    pre,
    gu_0,
    gu_1,
    gu_2,
    gu_3,
    partials,
    tiles,
    turned,
    sums,
    acc,
    tile_sems,
    sems,
):
    span = GROUPS // CHUNKS
    slot = pieces(place)
    zero_block = jnp.zeros((TILE, 128), F32)

    def load_turned(n):
        flat = pl.ds(n * span * DEPTH, span * DEPTH)
        return pltpu.make_async_copy(down_t.at[flat], turned.at[flat], sems.at[0, n])

    def store(n):
        rows = pl.ds(n * span, span)
        return pltpu.make_async_copy(sums.at[rows], partials.at[rows], sems.at[1, n])

    load_tiles = [tile_loads((gu_0, gu_1, gu_2, gu_3), tiles, tile_sems, n) for n in range(CHUNKS)]
    for n in range(CHUNKS):
        load_turned(n).start()
        for copy in load_tiles[n]:
            copy.start()

    for n in range(CHUNKS):
        load_turned(n).wait()
        for copy in load_tiles[n]:
            copy.wait()

        @pl.loop(n * span, (n + 1) * span, unroll=span)
        def _(q):
            for r in range(D_OWN):
                acc[0, r] = zero_block
                acc[1, r] = zero_block
            for base in range(0, DEPTH, 4):
                parts = []
                for c in range(base, base + 4):
                    k = q * DEPTH + c
                    parts.append(nn(turned[k], hidden_split[dmeta[0, k]]))
                for c in range(base, base + 4):
                    acc[0, dmeta[1, q * DEPTH + c]] += parts[c - base]
            for base in range(0, 2 * DEPTH, 4):
                parts = []
                for m in range(base, base + 4):
                    parts.append(nn(unpack(tiles[m, q]), pre[meta[q, 2 * DEPTH + slot[m]]]))
                for m in range(base, base + 4):
                    acc[1, meta[q, slot[m]]] += parts[m - base]
            for r in range(D_OWN):
                sums[q, 0, r] = acc[0, r].astype(BF)
                sums[q, 1, r] = acc[1, r].astype(BF)

        store(n).start()
    for n in range(CHUNKS):
        store(n).wait()


def turn_back_kernel(summed, layer_output, grad_tokens, held, ordered, sems):
    width = D_OWN * TILE

    def load(half):
        rows = pl.ds(half * width, width)
        return pltpu.make_async_copy(summed.at[rows], held.at[rows], sems.at[half])

    load(1).start()
    load(0).start()
    load(1).wait()
    for r in range(D_OWN):
        for odd in range(2):
            rows = held[pl.ds(width + r * TILE + odd * HALF, HALF), :]
            ordered[pl.ds(r * TILE + odd, HALF, stride=2), :] = rows.astype(F32)
    for n in range(width // 128):
        lanes = pl.ds(n * 128, 128)
        grad_tokens[:, lanes] = ordered[lanes, :].T.astype(BF)
    load(0).wait()
    for n in range(width // 128):
        lanes = pl.ds(n * 128, 128)
        layer_output[:, lanes] = held[lanes, :].T


def place_kernel(place, full_0, full_1, full_2, full_3, gate, up, down, sems):
    full = (full_0, full_1, full_2, full_3)
    for phase in range(2):
        for k in range(SIDE):
            first = (place[0] + SIDE - k) & (SIDE - 1)
            for j in range(SIDE):
                second = (place[1] + SIDE - j) & (SIDE - 1)
                slot = SIDE * k + j
                to_down = pltpu.make_async_copy(
                    full[k].at[j, pl.ds(GROUPS, DEPTH)], down.at[SIDE * first + second], sems.at[1, slot]
                )
                depth = SIDE * (first & 1) + second
                source = full[k].at[j, pl.ds(0, GROUPS)]
                to_gate = pltpu.make_async_copy(source, gate.at[:, depth], sems.at[0, slot])
                to_up = pltpu.make_async_copy(source, up.at[:, depth], sems.at[0, slot])
                for copy, when in ((to_gate, first < 2), (to_up, first >= 2)):

                    @pl.when(when)
                    def _(copy=copy):
                        if phase == 0:
                            copy.start()
                        else:
                            copy.wait()

                if phase == 0:
                    to_down.start()
                else:
                    to_down.wait()


SMEM = pl.BlockSpec(memory_space=pltpu.SMEM)
VMEM = pl.BlockSpec(memory_space=pltpu.VMEM)
ANY = pl.BlockSpec(memory_space=pl.ANY)
LIMIT = 48 * 1024 * 1024
SMALL = 16 * 1024 * 1024


def turn(down):
    whole = (GROUPS * DEPTH, TILE, TILE)
    return pl.pallas_call(
        turn_kernel,
        out_shape=jax.ShapeDtypeStruct(whole, BF),
        in_specs=[VMEM],
        out_specs=ANY,
        scratch_shapes=[pltpu.VMEM(whole, BF), pltpu.SemaphoreType.DMA((CHUNKS,))],
        compiler_params=pltpu.CompilerParams(vmem_limit_bytes=LIMIT),
        cost_estimate=pl.CostEstimate(flops=2**26, bytes_accessed=2**22, transcendentals=0),
        name="turn_kernel",
    )(down)


def layer(place, meta, dmeta, act, down, gu):
    block = (GROUPS, D_OWN, TILE, 128)
    piece = jax.ShapeDtypeStruct((SIDE, 3 * DEPTH, HALF, 128), BF)
    *grads, hidden_split, pre = pl.pallas_call(
        layer_kernel,
        out_shape=(piece,) * SIDE
        + (
            jax.ShapeDtypeStruct((F_OWN, TILE, 128), BF),
            jax.ShapeDtypeStruct((2 * F_OWN, TILE, 128), BF),
        ),
        in_specs=[SMEM, SMEM, SMEM, ANY, VMEM] + [ANY] * SIDE,
        out_specs=(ANY,) * SIDE + (VMEM, VMEM),
        scratch_shapes=[
            pltpu.VMEM(block, BF),
            pltpu.VMEM((2 * DEPTH, GROUPS, HALF, 128), BF),
            pltpu.VMEM(block, BF),
            pltpu.VMEM(block, BF),
            pltpu.VMEM((GROUPS, 3 * DEPTH, HALF, 128), BF),
            pltpu.VMEM((2 * F_OWN, 128, TILE), F32),
            pltpu.VMEM((F_OWN, TILE, 128), F32),
            pltpu.VMEM((F_OWN, TILE, 128), F32),
            pltpu.SemaphoreType.DMA((SIDE, CHUNKS)),
            pltpu.SemaphoreType.DMA((5, CHUNKS)),
        ],
        compiler_params=pltpu.CompilerParams(vmem_limit_bytes=LIMIT),
        cost_estimate=pl.CostEstimate(flops=2**29, bytes_accessed=2**23, transcendentals=0),
        name="layer_kernel",
    )(place, meta, dmeta, act, down, *gu)
    return grads, hidden_split, pre


def output_part(place, meta, dmeta, down_t, hidden_split, pre, gu):
    return pl.pallas_call(
        output_kernel,
        out_shape=jax.ShapeDtypeStruct((GROUPS, 2, D_OWN, TILE, 128), BF),
        in_specs=[SMEM, SMEM, SMEM, ANY, VMEM, VMEM] + [ANY] * SIDE,
        out_specs=ANY,
        scratch_shapes=[
            pltpu.VMEM((2 * DEPTH, GROUPS, HALF, 128), BF),
            pltpu.VMEM((GROUPS * DEPTH, TILE, TILE), BF),
            pltpu.VMEM((GROUPS, 2, D_OWN, TILE, 128), BF),
            pltpu.VMEM((2, D_OWN, TILE, 128), F32),
            pltpu.SemaphoreType.DMA((SIDE, CHUNKS)),
            pltpu.SemaphoreType.DMA((2, CHUNKS)),
        ],
        compiler_params=pltpu.CompilerParams(vmem_limit_bytes=LIMIT),
        cost_estimate=pl.CostEstimate(flops=2**28, bytes_accessed=2**23, transcendentals=0),
        name="output_kernel",
    )(place, meta, dmeta, down_t, hidden_split, pre, *gu)


def place_grads(place, full):
    tiles = jax.ShapeDtypeStruct((GROUPS, DEPTH, HALF, 128), BF)
    return pl.pallas_call(
        place_kernel,
        out_shape=(tiles,) * 3,
        in_specs=[SMEM] + [ANY] * SIDE,
        out_specs=(ANY,) * 3,
        scratch_shapes=[pltpu.SemaphoreType.DMA((2, SIDE * SIDE))],
        compiler_params=pltpu.CompilerParams(vmem_limit_bytes=SMALL),
        cost_estimate=pl.CostEstimate(flops=0, bytes_accessed=2**22, transcendentals=0),
        name="place_kernel",
    )(place, *full)


def turn_back(summed):
    width = D_OWN * TILE
    rows = jax.ShapeDtypeStruct((128, width), BF)
    return pl.pallas_call(
        turn_back_kernel,
        out_shape=(rows,) * 2,
        in_specs=[ANY],
        out_specs=(VMEM,) * 2,
        scratch_shapes=[
            pltpu.VMEM((2 * width, 128), BF),
            pltpu.VMEM((width, 128), F32),
            pltpu.SemaphoreType.DMA((2,)),
        ],
        compiler_params=pltpu.CompilerParams(vmem_limit_bytes=60 * 1024 * 1024),
        cost_estimate=pl.CostEstimate(flops=0, bytes_accessed=2**19, transcendentals=0),
        name="turn_back_kernel",
    )(summed)


def split_order(size):
    n = jnp.arange(size, dtype=jnp.int32)
    block, inner = n // TILE, n % TILE
    source = block * TILE + 2 * (inner % HALF) + inner // HALF
    return (source[:, None] == n[None, :]).astype(BF)


def lines(second):
    groups = []
    for mp in range(GROUPS):
        for other in range(SIDE):
            along_x = (mp % 2 == 0) != second
            groups.append(
                [
                    ((n * SIDE + other) if along_x else (other * SIDE + n)) * GROUPS + mp
                    for n in range(SIDE)
                ]
            )
    return groups


def shift(value, second, count):
    pairs = [
        (line[n], line[(n + count) % SIDE]) for line in lines(second) for n in range(SIDE)
    ]
    return lax.ppermute(value, ("dp", "mp"), pairs)


def to_replicas(piece):
    row = jnp.stack([piece] + [shift(piece, True, k) for k in range(1, SIDE)])
    return [row] + [shift(row, False, k) for k in range(1, SIDE)]


def from_replicas(rows, second):
    ahead = [
        lax.dynamic_index_in_dim(rows, (second + k) % SIDE, 0, keepdims=False)
        for k in range(SIDE)
    ]
    got = [ahead[0]] + [shift(ahead[k], True, k) for k in range(1, SIDE)]
    return [
        sum(part[rows].astype(F32) for part in got).astype(BF)
        for rows in (slice(0, GROUPS), slice(GROUPS, None))
    ]


def per_device(
    tokens,
    gate_tiles,
    gate_index,
    gate_count,
    up_tiles,
    up_index,
    up_count,
    down_tiles,
    down_index,
    down_count,
    grad_output,
):
    me = lax.axis_index("mp")
    replica = lax.axis_index("dp")
    crossed = me % 2
    turned = (replica % SIDE) * SIDE + replica // SIDE
    part = jnp.where(crossed == 1, turned, replica)
    place = jnp.stack([part // SIDE, part % SIDE]).astype(jnp.int32)
    width = tokens.shape[1]
    order = split_order(width)
    eye = jnp.eye(width, dtype=BF)
    groups = jnp.arange(GROUPS, dtype=jnp.int32)[:, None]
    slots = jnp.arange(DEPTH, dtype=jnp.int32)[None, :]

    tokens_t = jnp.einsum("pi,ti->pt", order, tokens, preferred_element_type=F32).astype(BF)
    grad_t = jnp.einsum("pi,ti->pt", eye, grad_output, preferred_element_type=F32).astype(BF)
    tokens_p = jnp.einsum("ti,pi->tp", tokens, order, preferred_element_type=F32).astype(BF)
    tokens_p = tokens_p.reshape(128, width // 128, 128).transpose(1, 0, 2).reshape(width, 128)
    own = jnp.concatenate([tokens_t, grad_t, tokens_p], axis=0)
    own, gate_index, up_index, gate_tiles, up_tiles = lax.optimization_barrier(
        (own, gate_index, up_index, gate_tiles, up_tiles)
    )
    act = lax.all_gather(own, "mp", axis=0)
    act = act.reshape(GROUPS, 3, D_OWN, TILE, 128)

    def blocks(index):
        return index.reshape(GROUPS, DEPTH, 2)

    is_up = part // DEPTH
    depth = part % DEPTH
    gate_t = lax.dynamic_index_in_dim(
        gate_tiles.reshape(GROUPS, DEPTH, HALF, 128), depth, 1, keepdims=False
    )
    up_t = lax.dynamic_index_in_dim(
        up_tiles.reshape(GROUPS, DEPTH, HALF, 128), depth, 1, keepdims=False
    )
    count = jnp.where(is_up == 1, up_count, gate_count)
    my_live = (depth < count)[:, None, None]
    mine = jnp.where(my_live, jnp.where(is_up == 1, up_t, gate_t), 0)
    gate_b, up_b = blocks(gate_index), blocks(up_index)
    notes = jnp.concatenate(
        [
            gate_b[..., 0] - me * D_OWN,
            up_b[..., 0] - me * D_OWN,
            gate_b[..., 1] - groups * F_OWN,
            up_b[..., 1] - groups * F_OWN + F_OWN,
        ],
        axis=1,
    ).astype(BF)
    notes = jnp.pad(notes[:, None, :], ((0, 0), (0, 7), (0, 128 - 4 * DEPTH)))
    sent = lax.all_to_all(
        jnp.concatenate([mine, notes], axis=1), "mp", 0, 0, tiled=True
    )
    meta = sent[:, HALF, : 4 * DEPTH].astype(jnp.int32).reshape(GROUPS, 2, SIDE, SIDE)
    same = (groups % 2 == crossed)[..., None, None]
    meta = jnp.where(same, meta, meta.swapaxes(2, 3)).reshape(GROUPS, 4 * DEPTH)
    gu = to_replicas(sent[:, :HALF])

    down_b = blocks(down_index)
    down_live = slots < down_count[:, None]
    dmeta = jnp.stack(
        [
            (down_b[..., 0] - me * F_OWN).reshape(-1),
            (down_b[..., 1] - groups * D_OWN).reshape(-1),
            down_live.astype(jnp.int32).reshape(-1),
        ]
    )
    down = jnp.where(
        down_live.reshape(-1)[:, None, None], down_tiles.reshape(GROUPS * DEPTH, HALF, 128), 0
    )

    down_t = turn(down)
    down, down_t = lax.optimization_barrier((down, down_t))
    grads, hidden_split, pre = layer(place, meta, dmeta, act, down, gu)
    grads = [grads[0]] + [shift(grads[k], False, k) for k in range(1, SIDE)]
    partials = output_part(place, meta, dmeta, down_t, hidden_split, pre, gu)
    rows = sum(part.astype(F32) for part in grads).astype(BF)
    rows, partials = lax.optimization_barrier((rows, partials))

    summed = lax.psum_scatter(
        partials.reshape(GROUPS * 2 * width, 128), "mp", scatter_dimension=0, tiled=True
    )

    got_gu, got_down = from_replicas(rows, part % SIDE)
    back = lax.all_to_all(got_gu, "mp", 0, 0, tiled=True)
    piece = jnp.concatenate([jnp.where(my_live, back, 0), got_down], axis=0)
    flat = (GROUPS * DEPTH * HALF, 128)
    tile_grads = place_grads(place, to_replicas(piece))
    layer_output, grad_tokens = turn_back(summed)
    grad_gate, grad_up, grad_down = (g.reshape(flat) for g in tile_grads)
    return (layer_output, grad_tokens, grad_gate, grad_up, grad_down)


def solution(mesh):
    return jax.shard_map(
        per_device,
        mesh=mesh,
        in_specs=(
            P("dp", "mp"),
            P("mp", None),
            P("mp", None),
            P("mp"),
            P("mp", None),
            P("mp", None),
            P("mp"),
            P("mp", None),
            P("mp", None),
            P("mp"),
            P("dp", "mp"),
        ),
        out_specs=(P("dp", "mp"), P("dp", "mp"), P("mp", None), P("mp", None), P("mp", None)),
        check_vma=False,
    )
```
